32 devices in a mesh: group: 2 (over x), flux: 8 (over z, y), obs: 2 (over core).
Axes of the slice: x: 2, y: 2, z: 4, core: 2. Of those that a mesh axis runs over, the one named last changes fastest.
Arguments:
- footprints: bfloat16 [16, 2, 6, 128, 24, 128], P(('group', 'flux'), 'obs'), parts along dimension 0, may hold values from -0.109375 to 0.109375
- slot_target: int32 [16, 2, 6], P(('group', 'flux'), 'obs'), parts along dimension 0, may hold values from 0 to 9
- slot_count: int32 [16, 2], P(('group', 'flux'), 'obs'), parts along dimension 0, may hold values from 1 to 6, as said below
- step_count: int32 [128], P(('group', 'obs')), parts along dimension 0, may hold values from 1 to 4, as said below
- sigma: float32 [48, 1024], P('group', 'flux'), parts along dimension 0, may hold values from 0.3 to 3
- innovations: float32 [64, 64, 128], P(('group', 'flux', 'obs')), parts along dimension 0, may hold values from -6 to 6
- obs_weight: float32 [64, 128], P(('group', 'flux', 'obs')), parts along dimension 0, may hold values from 0.25 to 4
Outputs:
- increment: float32 [128, 24, 1024], P(('group', 'obs'), None, 'flux'), parts along dimension 0
- residual: float32 [128, 24, 1024], P(('group', 'obs'), None, 'flux'), parts along dimension 0
The draws below stay inside these ranges and needn't reach their ends.
There are 2 independent parts, one for each index of `group`. The reference program is written for one: setup_inputs(seed, part) draws one part's arguments, and reference() takes and returns one part's arrays. A program takes and returns all parts, laid end to end along the dimension named above; each array names one. Nothing has to cross between parts.
Inputs may be any that keep to these rules, and one draw needn't show every extreme that they name: slot_target[f, o, s] = (d + 2) * 2 + j names block j of the device d flux indices away (mod 8) with the same obs index. The first slot_count[f, o] slots of a device are live; some device has all 6 live and some only one. `step_count`: some member takes 4 steps and some one.
All inputs are finite; a program needn't handle non-finite values.
Results may differ from the reference program's by a relative error of at most 0.0077.
Values may be sent and summed in bfloat16 or wider, within the bound.
No kernel may reach another device: no remote copies, remote signals or barrier semaphores. Data moves between devices by JAX's collectives and lax.ppermute only.
A program may use at most 64 MiB of HBM per device.

```python
import math
import jax
import jax.numpy as jnp
from jax import lax

NLAT = 24
LON_DEV = 128
OBLK = 128
SLOTS = 6
BLK_DEV = 2
REACH = 2
KMAX = 4
ITERS = 2
ENS = 64
NLON = 1024
OBS_BLOCKS = 32
N_FLUX = 8
N_OBS = 2


def spread_ints(key, total, highest):
    values = jax.random.randint(key, (total,), 1, highest + 1)
    first = jax.random.randint(jax.random.fold_in(key, 1), (), 0, total)
    second = (first + 1 + jax.random.randint(jax.random.fold_in(key, 2), (), 0, total - 1)) % total
    places = jnp.arange(total)
    values = jnp.where(places == first, highest, values)
    values = jnp.where(places == second, 1, values)
    return values.astype(jnp.int32)


def draw_slot_count(key, part):
    key = jax.random.fold_in(key, 5)
    return spread_ints(key, N_FLUX * N_OBS, SLOTS).reshape(N_FLUX, N_OBS)


def draw_step_count(key, part):
    key = jax.random.fold_in(key, 9)
    return spread_ints(key, ENS, KMAX)


def with_ends(entries, key, low, high):
    extent = entries.shape
    spot = [jax.random.randint(jax.random.fold_in(key, axis), (), 0, extent[axis]) for axis in range(len(extent))]
    entries = entries.at[tuple(spot)].set(low)
    longest = extent.index(max(extent))
    spot[longest] = (spot[longest] + 1) % extent[longest]
    return entries.at[tuple(spot)].set(high)


def block_levels(own_key, dims, cuts, least, largest):
    def one(dim, shards_of):
        heights = jax.random.uniform(jax.random.fold_in(jax.random.fold_in(own_key, 6), dim), (shards_of,), jnp.float32, least / len(cuts), largest / len(cuts))
        return jnp.repeat(jnp.exp(heights), dims[dim] // shards_of).reshape((-1,) + (1,) * (len(dims) - dim - 1))

    level = one(*cuts[0])
    for cut in cuts[1:]:
        level = level * one(*cut)
    return level


def normal_values(rng, shape, deviation, limit, pieces=(), held_as=jnp.bfloat16):
    result = jax.random.normal(rng, shape, jnp.float32) * deviation
    if len(pieces) > 0:
        result = block_levels(rng, shape, pieces, -0.22, 0.18) * result
    return jnp.clip(result, min=-limit, max=limit).astype(held_as)


def setup_inputs(seed: int = 0, part: int = 0) -> dict:
    key_list = jax.random.split(jax.random.key(seed), 8)
    part_splits = jax.random.split(jax.random.fold_in(key_list[7], part), 8)
    footprints = normal_values(part_splits[0], (N_FLUX, N_OBS, SLOTS, OBLK, NLAT, LON_DEV), (NLAT * LON_DEV) ** -0.5, 0.109375, ((0, 8), (1, 2)))
    slot_target = with_ends(jax.random.randint(part_splits[1], (N_FLUX, N_OBS, SLOTS), 0, (2 * REACH + 1) * BLK_DEV), jax.random.fold_in(part_splits[1], 1), 0, ((2 * REACH + 1) * BLK_DEV) - 1).astype(jnp.int32)
    slot_count = draw_slot_count(jax.random.fold_in(jax.random.fold_in(key_list[7], part), 71), part)
    step_count = draw_step_count(jax.random.fold_in(jax.random.fold_in(key_list[7], part), 71), part)
    sigma = jnp.clip(jnp.exp(math.log(3.0) - 2.3025851 * jax.random.uniform(part_splits[4], (NLAT, NLON), jnp.float32) ** block_levels(part_splits[4], (NLAT, NLON), ((1, 8),), -0.2, 0.2)), 0.3, 3.0)
    innovations = normal_values(part_splits[5], (OBS_BLOCKS, ENS, OBLK), 1.0, 6.0, ((0, 16),), jnp.float32)
    obs_weight = jnp.clip(jnp.exp(math.log(4.0) - 2.7725887 * jax.random.uniform(part_splits[6], (OBS_BLOCKS, OBLK), jnp.float32) ** block_levels(part_splits[6], (OBS_BLOCKS, OBLK), ((0, 16),), -0.2, 0.2)), 0.25, 4.0)
    return {"footprints": footprints, "slot_target": slot_target, "slot_count": slot_count, "step_count": step_count, "sigma": sigma, "innovations": innovations, "obs_weight": obs_weight}


spread_rate = 0.24


def diffuse(field, step_count):
    for step in range(KMAX):
        padded = jnp.pad(field, ((0, 0), (1, 1), (0, 0)))
        updated = field + spread_rate * (padded[:, :-2] + padded[:, 2:] + jnp.roll(field, 1, 2) + jnp.roll(field, -1, 2) - 4.0 * field)
        field = jnp.where((step < step_count)[:, None, None], updated, field)
    return field


def reference(footprints, slot_target, slot_count, step_count, sigma, innovations, obs_weight):
    flux_rows = jnp.arange(N_FLUX, dtype=jnp.int32)[:, None, None]
    obs_rows = jnp.arange(N_OBS, dtype=jnp.int32)[None, :, None]
    offset = slot_target // BLK_DEV - REACH
    target_block = ((((flux_rows + offset) % N_FLUX) * N_OBS + obs_rows) * BLK_DEV + slot_target % BLK_DEV).astype(jnp.int32)
    live_mask = (jnp.arange(SLOTS, dtype=jnp.int32)[None, None, :] < slot_count[:, :, None]).astype(jnp.float32)

    def forward(field):
        field_bf16 = field.astype(jnp.bfloat16).reshape(ENS, NLAT, N_FLUX, LON_DEV)
        bands = jnp.moveaxis(field_bf16, 2, 0)

        def project(pair):
            tiles, band_field = pair
            return jnp.einsum("osinl,enl->osei", tiles.astype(jnp.float32), band_field.astype(jnp.float32))

        slot_values = lax.map(project, (footprints, bands)) * live_mask[:, :, :, None, None]
        return jax.ops.segment_sum(slot_values.reshape(-1, ENS, OBLK), target_block.reshape(-1), num_segments=OBS_BLOCKS)

    def adjoint(weighted):
        picked = weighted[target_block].astype(jnp.float32) * live_mask[:, :, :, None, None]

        def project(pair):
            tiles, chosen = pair
            return jnp.einsum("osinl,osei->enl", tiles.astype(jnp.float32), chosen)

        terms = lax.map(project, (footprints, picked))
        return jnp.moveaxis(terms, 0, 2).reshape(ENS, NLAT, NLON)

    def weigh(values):
        return (obs_weight[:, None, :] * values).astype(jnp.bfloat16)

    def lower(field):
        return sigma[None] * diffuse(field, step_count)

    def upper(field):
        return diffuse(sigma[None] * field, step_count)

    def operate(direction):
        return direction + upper(adjoint(weigh(forward(lower(direction)))))

    right = upper(adjoint(weigh(innovations)))
    solution = jnp.zeros_like(right)
    residual = right
    direction = right
    norm_now = jnp.sum(residual * residual, axis=(1, 2))
    for turn in range(ITERS):
        image = operate(direction)
        step_size = norm_now / jnp.sum(direction * image, axis=(1, 2))
        solution = solution + step_size[:, None, None] * direction
        residual = residual - step_size[:, None, None] * image
        norm_next = jnp.sum(residual * residual, axis=(1, 2))
        direction = residual + (norm_next / norm_now)[:, None, None] * direction
        norm_now = norm_next
    return lower(solution), residual
```

```python
import functools

import jax
import jax.numpy as jnp
from jax import lax
from jax.experimental import pallas as pl
from jax.experimental.pallas import tpu as pltpu
from jax.sharding import PartitionSpec as P

REACH = 2
KMAX = 4
OFFSETS = 2 * REACH + 1
SPREAD = 0.24
F32 = jnp.float32
BF16 = jnp.bfloat16
VMEM_LIMIT = 48 * 1024 * 1024


def shifted(block, axis, distance):
    size = lax.axis_size(axis)
    return lax.ppermute(block, axis, [(i, (i + distance) % size) for i in range(size)])


def kernel_params(**more):
    return pltpu.CompilerParams(vmem_limit_bytes=VMEM_LIMIT, **more)


def vmem():
    return pl.BlockSpec(memory_space=pltpu.VMEM)


def smem():
    return pl.BlockSpec(memory_space=pltpu.SMEM)


def flatten_kernel(tile_ref, out_ref, wide):
    _, obs, lat, lon = tile_ref.shape
    for start in range(0, obs, 16):
        wide[pl.ds(start * lat, 16 * lat), :] = (
            tile_ref[0, pl.ds(start, 16)].astype(F32).reshape(16 * lat, lon)
        )
        for row in range(lat):
            part = wide[pl.ds(start * lat + row, 16, stride=lat), :]
            out_ref[pl.ds(start, 16), pl.ds(row * lon, lon)] = part.astype(BF16)


def flatten_tiles(tiles):
    slots, obs, lat, lon = tiles.shape
    return pl.pallas_call(
        flatten_kernel,
        out_shape=jax.ShapeDtypeStruct((slots * obs, lat * lon), BF16),
        grid=(slots,),
        in_specs=[pl.BlockSpec((1, obs, lat, lon), lambda s: (s, 0, 0, 0))],
        out_specs=pl.BlockSpec((obs, lat * lon), lambda s: (s, 0)),
        scratch_shapes=[pltpu.VMEM((obs * lat, lon), F32)],
        compiler_params=kernel_params(),
        cost_estimate=pl.CostEstimate(flops=0, bytes_accessed=4 * tiles.size, transcendentals=0),
        name="flatten_tiles",
    )(tiles)


def split(value):
    high = value.astype(BF16)
    return high, (value - high.astype(F32)).astype(BF16)


def adjoint_kernel(edge, target_ref, live_ref, *refs):
    pieces = refs[:OFFSETS]
    own_ref, other_ref, sigma_ref, field_ref, first_ref, last_ref, near, picked = refs[OFFSETS:]
    count, members, obs = pieces[0].shape
    slots = own_ref.shape[0] // obs
    lat, lon = sigma_ref.shape
    for offset in range(OFFSETS):
        near[pl.ds(offset * count, count)] = pieces[offset][...].astype(F32)
    for side in range(2):
        for slot in range(slots):
            target = target_ref[side, slot]
            block = near[(target // 2) * count + side * 2 + target % 2] * live_ref[side, slot]
            high, low = split(block)
            columns = pl.ds((side * slots + slot) * obs, obs)
            picked[pl.ds(0, members), columns] = high
            picked[pl.ds(members, members), columns] = low
    half = slots * obs
    for row in range(0, lat, 2):
        cells = pl.ds(row * lon, 2 * lon)
        both = jnp.dot(picked[:, :half], own_ref[:, cells], preferred_element_type=F32)
        both = both + jnp.dot(picked[:, half:], other_ref[:, cells], preferred_element_type=F32)
        total = both[:members] + both[members:]
        for k in range(2):
            field = total[:, k * lon : (k + 1) * lon] * sigma_ref[row + k, :][None, :]
            field_ref[row + k] = field
            first_ref[:, pl.ds((row + k) * edge, edge)] = field[:, :edge]
            last_ref[:, pl.ds((row + k) * edge, edge)] = field[:, lon - edge :]


def adjoint(pieces, targets, live, own, other, sigma, edge):
    count, members, obs = pieces[0].shape
    lat, lon = sigma.shape
    return pl.pallas_call(
        functools.partial(adjoint_kernel, edge),
        out_shape=(
            jax.ShapeDtypeStruct((lat, members, lon), F32),
            jax.ShapeDtypeStruct((members, lat * edge), F32),
            jax.ShapeDtypeStruct((members, lat * edge), F32),
        ),
        in_specs=[smem(), smem()] + [vmem()] * (OFFSETS + 3),
        out_specs=(vmem(), vmem(), vmem()),
        scratch_shapes=[
            pltpu.VMEM((OFFSETS * count, members, obs), F32),
            pltpu.VMEM((2 * members, 2 * own.shape[0]), BF16),
        ],
        compiler_params=kernel_params(),
        cost_estimate=pl.CostEstimate(
            flops=8 * members * own.size, bytes_accessed=4 * own.size, transcendentals=0
        ),
        name="adjoint",
    )(targets, live, *pieces, own, other, sigma)


def spread_steps(rows, coefs):
    zero = jnp.zeros_like(rows[0])
    lanes = rows[0].shape[1]
    for coef in coefs:
        keep = 1.0 - 4.0 * coef
        padded = [zero] + rows + [zero]
        rows = [
            keep * padded[i]
            + coef
            * (
                (padded[i - 1] + padded[i + 1])
                + (pltpu.roll(padded[i], 1, 1) + pltpu.roll(padded[i], lanes - 1, 1))
            )
            for i in range(1, len(rows) + 1)
        ]
    return rows


def extended_rows(field_ref, first_ref, last_ref, edge, group):
    lat, _, lon = field_ref.shape
    rows = []
    for row in range(lat):
        after = first_ref[group, pl.ds(row * edge, edge)]
        before = last_ref[group, pl.ds(row * edge, edge)]
        gap = jnp.zeros((8, lon - 2 * edge), F32)
        rows.append(jnp.concatenate([field_ref[row, group, :], after, gap, before], axis=1))
    return rows


def coefficients(steps_ref, group):
    steps = steps_ref[group, :]
    return [jnp.where(step < steps, SPREAD, 0.0).astype(F32) for step in range(KMAX)]


def forward_kernel(edge, second, target_ref, live_ref, *refs):
    field_ref, first_ref, last_ref, steps_ref, sigma_ref, own_ref, other_ref = refs[:7]
    refs = refs[7:]
    if second:
        before_ref, refs = refs[0], refs[1:]
    upper_ref, lower_ref, dots_ref = refs[:3]
    pieces = refs[3 : 3 + OFFSETS]
    halves, sums = refs[3 + OFFSETS :]
    lat, members, lon = field_ref.shape
    obs = sums.shape[2]
    slots = own_ref.shape[0] // obs
    count = pieces[0].shape[0]

    @pl.loop(0, members // 8)
    def _(index):
        group = pl.ds(pl.multiple_of(index * 8, 8), 8)
        coefs = coefficients(steps_ref, group)
        rows = extended_rows(field_ref, first_ref, last_ref, edge, group)
        rows = spread_steps(rows, coefs)
        square = jnp.zeros((8, lon), F32)
        cross = jnp.zeros((8, lon), F32)
        for row in range(lat):
            own_cells = rows[row][:, :lon]
            upper_ref[row, group, :] = own_cells
            square = square + own_cells * own_cells
            if second:
                cross = cross + own_cells * before_ref[row, group, :]
        dots_ref[0, group, :] = square
        if second:
            dots_ref[1, group, :] = cross
        rows = spread_steps(rows, coefs)
        for row in range(lat):
            low_field = rows[row][:, :lon] * sigma_ref[row, :][None, :]
            lower_ref[row, group, :] = low_field

    for row in range(lat):
        high, low = split(lower_ref[row])
        halves[pl.ds(0, members), pl.ds(row * lon, lon)] = high
        halves[pl.ds(members, members), pl.ds(row * lon, lon)] = low
    sums[...] = jnp.zeros_like(sums)
    contract = (((1,), (1,)), ((), ()))
    for side, tile_ref in enumerate((own_ref, other_ref)):
        for slot in range(0, slots, 2):
            both = lax.dot_general(
                halves[...], tile_ref[pl.ds(slot * obs, 2 * obs), :], contract, preferred_element_type=F32
            )
            total = both[:members] + both[members:]
            for k in range(2):
                target = target_ref[side, slot + k]
                place = (target // 2) * count + side * 2 + target % 2
                sums[place] = sums[place] + total[:, k * obs : (k + 1) * obs] * live_ref[side, slot + k]
    for offset in range(OFFSETS):
        pieces[offset][...] = sums[pl.ds(offset * count, count)]


def forward(field, first, last, steps, sigma, own, other, targets, live, count, edge, before=None):
    lat, members, lon = field.shape
    obs = own.shape[0] // targets.shape[1]
    more = () if before is None else (before,)
    shape = jax.ShapeDtypeStruct((lat, members, lon), F32)
    piece = jax.ShapeDtypeStruct((count, members, obs), F32)
    dots = jax.ShapeDtypeStruct((1 + len(more), members, lon), F32)
    return pl.pallas_call(
        functools.partial(forward_kernel, edge, before is not None),
        out_shape=(shape, shape, dots) + (piece,) * OFFSETS,
        in_specs=[smem(), smem()] + [vmem()] * (7 + len(more)),
        out_specs=(vmem(),) * (3 + OFFSETS),
        scratch_shapes=[
            pltpu.VMEM((2 * members, lat * lon), BF16),
            pltpu.VMEM((OFFSETS * count, members, obs), F32),
        ],
        compiler_params=kernel_params(),
        cost_estimate=pl.CostEstimate(
            flops=8 * members * own.size, bytes_accessed=4 * own.size, transcendentals=0
        ),
        name="forward",
    )(targets, live, field, first, last, steps, sigma, own, other, *more)


def finish_kernel(edge, field_ref, first_ref, last_ref, steps_ref, dots_ref, *refs):
    start_ref, image_ref, start_low_ref, image_low_ref, increment_ref, residual_ref = refs
    lat, members, lon = field_ref.shape

    @pl.loop(0, members // 8)
    def _(index):
        group = pl.ds(pl.multiple_of(index * 8, 8), 8)
        coefs = coefficients(steps_ref, group)
        rows = extended_rows(field_ref, first_ref, last_ref, edge, group)
        rows = spread_steps(rows, coefs)
        pp, pg, gg, gh = [dots_ref[group, pl.ds(k, 1)] for k in range(4)]
        step0 = pp / (pp + pg)
        u, w = 1.0 - step0, -step0
        norm1 = u * u * pp + 2.0 * u * w * pg + w * w * gg
        x = u + norm1 / pp
        curve = x * (x * pp + (x + w) * pg + w * gg) + w * (x * pg + (x + w) * gg + w * gh)
        step1 = norm1 / curve
        inc_p, inc_g = step0 + step1 * x, step1 * w
        res_p, res_g, res_h = u - step1 * x, w - step1 * (x + w), -step1 * w
        for row in range(lat):
            increment_ref[group, row, :] = (
                inc_p * start_low_ref[row, group, :] + inc_g * image_low_ref[row, group, :]
            )
            residual_ref[group, row, :] = (
                res_p * start_ref[row, group, :]
                + res_g * image_ref[row, group, :]
                + res_h * rows[row][:, :lon]
            )


def finish(field, first, last, steps, dots, start, image, start_low, image_low, edge):
    lat, members, lon = field.shape
    out = jax.ShapeDtypeStruct((members, lat, lon), F32)
    return pl.pallas_call(
        functools.partial(finish_kernel, edge),
        out_shape=(out, out),
        in_specs=[vmem()] * 9,
        out_specs=(vmem(), vmem()),
        compiler_params=kernel_params(),
        name="finish",
    )(field, first, last, steps, dots, start, image, start_low, image_low)


def local(footprints, slot_target, slot_count, step_count, sigma, innovations, obs_weight):
    tiles = footprints[0, 0]
    slots, obs, lat, lon = tiles.shape
    blocks, ensemble, _ = innovations.shape
    members = step_count.shape[0]
    mine = lax.axis_index("obs")
    steps = step_count[:, None]
    live = (jnp.arange(slots, dtype=jnp.int32) < slot_count[0, 0]).astype(F32)
    weighted = (obs_weight[:, None, :] * innovations).astype(BF16).astype(F32)
    kept = lax.dynamic_slice_in_dim(weighted, mine * members, members, 1)
    given = lax.dynamic_slice_in_dim(weighted, (1 - mine) * members, members, 1)
    facts = jnp.concatenate([slot_target[0, 0].astype(F32), live, jnp.zeros((obs - 2 * slots,), F32)])
    packet = jnp.concatenate([given.reshape(-1, obs), obs_weight, facts[None]])
    got = shifted(packet, "obs", 1)
    rows = blocks * members
    given = got[:rows].reshape(blocks, members, obs)
    weight = jnp.concatenate([obs_weight, got[rows : rows + blocks]])
    facts = jnp.stack([facts, got[rows + blocks]])
    targets = facts[:, :slots].astype(jnp.int32)
    live = facts[:, slots : 2 * slots]
    start_blocks = jnp.concatenate([kept, given]).astype(BF16)
    count = 2 * blocks

    other = flatten_tiles(shifted(tiles, "obs", 1))
    own = flatten_tiles(tiles)

    def nearby(block):
        return [block if k == REACH else shifted(block, "flux", REACH - k) for k in range(OFFSETS)]

    def back(block, edge):
        field, first, last = adjoint(nearby(block), targets, live, own, other, sigma, edge)
        return field, shifted(first, "flux", -1), shifted(last, "flux", 1)

    def home(pieces):
        total = pieces[REACH]
        for k in range(OFFSETS):
            if k != REACH:
                total = total + shifted(pieces[k], "flux", k - REACH)
        return total

    wide = 2 * KMAX
    field, first, last = back(start_blocks, wide)
    start, start_low, dots, *pieces = forward(
        field, first, last, steps, sigma, own, other, targets, live, count, wide
    )
    pp = jnp.sum(dots[0], axis=1)
    field, first, last = back(weight[:, None, :] * home(pieces), wide)
    image, image_low, dots, *pieces = forward(
        field, first, last, steps, sigma, own, other, targets, live, count, wide, start
    )
    gg, pg = jnp.sum(dots[0], axis=1), jnp.sum(dots[1], axis=1)
    total = home(pieces)
    weighted = weight[:, None, :] * total
    gh = jnp.sum(total * weighted, axis=(0, 2))
    products = lax.psum(jnp.stack([pp, pg, gg, gh]), "flux").T
    field, first, last = back(weighted, KMAX)
    return finish(field, first, last, steps, products, start, image, start_low, image_low, KMAX)


def solution(mesh):
    return jax.shard_map(
        local,
        mesh=mesh,
        in_specs=(
            P(("group", "flux"), "obs", None, None, None, None),
            P(("group", "flux"), "obs", None),
            P(("group", "flux"), "obs"),
            P(("group", "obs")),
            P("group", "flux"),
            P(("group", "flux", "obs"), None, None),
            P(("group", "flux", "obs"), None),
        ),
        out_specs=(P(("group", "obs"), None, "flux"), P(("group", "obs"), None, "flux")),
        check_vma=False,
    )
```

```python
import functools

import jax
import jax.numpy as jnp
from jax import lax
from jax.experimental import pallas as pl
from jax.experimental.pallas import tpu as pltpu
from jax.sharding import PartitionSpec as P

REACH = 2
KMAX = 4
OFFSETS = 2 * REACH + 1
SPREAD = 0.24
F32 = jnp.float32
BF16 = jnp.bfloat16
VMEM_LIMIT = 16 * 1024 * 1024
STRIDE = 3


def shifted(block, axis, distance):
    size = lax.axis_size(axis)
    return lax.ppermute(block, axis, [(i, (i + distance) % size) for i in range(size)])


def kernel_params(**more):
    return pltpu.CompilerParams(vmem_limit_bytes=VMEM_LIMIT, **more)


def vmem():
    return pl.BlockSpec(memory_space=pltpu.VMEM)


def smem():
    return pl.BlockSpec(memory_space=pltpu.SMEM)


def flatten_kernel(pitch, tile_ref, out_ref, wide):
    _, obs, lat, lon = tile_ref.shape
    for start in range(0, obs, 16):
        side = start // 16 % 2
        for k in range(16):
            wide[side, pl.ds(k * pitch, lat, stride=STRIDE), :] = tile_ref[0, start + k].astype(F32)
        for row in range(lat):
            part = wide[side, pl.ds(row * STRIDE, 16, stride=pitch), :]
            out_ref[pl.ds(start, 16), pl.ds(row * lon, lon)] = part.astype(BF16)


def flatten_tiles(tiles):
    slots, obs, lat, lon = tiles.shape
    pitch = (lat * STRIDE) | 1
    return pl.pallas_call(
        functools.partial(flatten_kernel, pitch),
        out_shape=jax.ShapeDtypeStruct((slots * obs, lat * lon), BF16),
        grid=(slots,),
        in_specs=[pl.BlockSpec((1, obs, lat, lon), lambda s: (s, 0, 0, 0))],
        out_specs=pl.BlockSpec((obs, lat * lon), lambda s: (s, 0)),
        scratch_shapes=[pltpu.VMEM((2, 16 * pitch, lon), F32)],
        compiler_params=kernel_params(),
        cost_estimate=pl.CostEstimate(flops=0, bytes_accessed=4 * tiles.size, transcendentals=0),
        name="flatten_tiles",
    )(tiles)


def split(value):
    high = value.astype(BF16)
    return high, (value - high.astype(F32)).astype(BF16)


def adjoint_kernel(edge, target_ref, live_ref, *refs):
    pieces = refs[:OFFSETS]
    own_ref, other_ref, sigma_ref, field_ref, first_ref, last_ref, near, picked = refs[OFFSETS:]
    members = picked.shape[0] // 2
    obs = pieces[0].shape[1]
    rows = near.shape[0] // OFFSETS
    count = rows // members
    slots = own_ref.shape[0] // obs
    lat, lon = sigma_ref.shape
    for offset in range(OFFSETS):
        near[pl.ds(offset * rows, rows), :] = pieces[offset][pl.ds(0, rows), :].astype(F32)
    for side in range(2):
        for slot in range(slots):
            target = target_ref[side, slot]
            place = (target // 2) * count + side * 2 + target % 2
            block = near[pl.ds(pl.multiple_of(place * members, members), members), :] * live_ref[side, slot]
            high, low = split(block)
            columns = pl.ds((side * slots + slot) * obs, obs)
            picked[pl.ds(0, members), columns] = high
            picked[pl.ds(members, members), columns] = low
    half = slots * obs
    for row in range(0, lat, 2):
        cells = pl.ds(row * lon, 2 * lon)
        both = jnp.dot(picked[:, :half], own_ref[:, cells], preferred_element_type=F32)
        both = both + jnp.dot(picked[:, half:], other_ref[:, cells], preferred_element_type=F32)
        total = both[:members] + both[members:]
        for k in range(2):
            field = total[:, k * lon : (k + 1) * lon] * sigma_ref[row + k, :][None, :]
            field_ref[row + k] = field
            first_ref[:, pl.ds((row + k) * edge, edge)] = field[:, :edge]
            last_ref[:, pl.ds((row + k) * edge, edge)] = field[:, lon - edge :]


def adjoint(pieces, targets, live, own, other, sigma, count, members, edge):
    obs = pieces[0].shape[1]
    lat, lon = sigma.shape
    return pl.pallas_call(
        functools.partial(adjoint_kernel, edge),
        out_shape=(
            jax.ShapeDtypeStruct((lat, members, lon), F32),
            jax.ShapeDtypeStruct((members, lat * edge), F32),
            jax.ShapeDtypeStruct((members, lat * edge), F32),
        ),
        in_specs=[smem(), smem()] + [vmem()] * (OFFSETS + 3),
        out_specs=(vmem(), vmem(), vmem()),
        scratch_shapes=[
            pltpu.VMEM((OFFSETS * count * members, obs), F32),
            pltpu.VMEM((2 * members, 2 * own.shape[0]), BF16),
        ],
        compiler_params=kernel_params(),
        cost_estimate=pl.CostEstimate(
            flops=8 * members * own.size, bytes_accessed=4 * own.size, transcendentals=0
        ),
        name="adjoint",
    )(targets, live, *pieces, own, other, sigma)


def spread_steps(rows, coefs):
    zero = jnp.zeros_like(rows[0])
    lanes = rows[0].shape[1]
    for coef in coefs:
        keep = 1.0 - 4.0 * coef
        padded = [zero] + rows + [zero]
        rows = [
            keep * padded[i]
            + coef
            * (
                (padded[i - 1] + padded[i + 1])
                + (pltpu.roll(padded[i], 1, 1) + pltpu.roll(padded[i], lanes - 1, 1))
            )
            for i in range(1, len(rows) + 1)
        ]
    return rows


def extended_rows(field_ref, first_ref, last_ref, edge, group):
    lat, _, lon = field_ref.shape
    rows = []
    for row in range(lat):
        after = first_ref[group, pl.ds(row * edge, edge)]
        before = last_ref[group, pl.ds(row * edge, edge)]
        gap = jnp.zeros((8, lon - 2 * edge), F32)
        rows.append(jnp.concatenate([field_ref[row, group, :], after, gap, before], axis=1))
    return rows


def coefficients(steps_ref, group):
    steps = steps_ref[group, :]
    return [jnp.where(step < steps, SPREAD, 0.0).astype(F32) for step in range(KMAX)]


def forward_kernel(edge, second, target_ref, live_ref, *refs):
    field_ref, first_ref, last_ref, steps_ref, sigma_ref, own_ref, other_ref = refs[:7]
    refs = refs[7:]
    if second:
        before_ref, refs = refs[0], refs[1:]
    upper_ref, lower_ref, dots_ref = refs[:3]
    pieces = refs[3 : 3 + OFFSETS]
    halves, sums = refs[3 + OFFSETS :]
    lat, members, lon = field_ref.shape
    obs = sums.shape[2]
    slots = own_ref.shape[0] // obs
    count = pieces[0].shape[0]

    @pl.loop(0, members // 8)
    def _(index):
        group = pl.ds(pl.multiple_of(index * 8, 8), 8)
        coefs = coefficients(steps_ref, group)
        rows = extended_rows(field_ref, first_ref, last_ref, edge, group)
        rows = spread_steps(rows, coefs)
        square = jnp.zeros((8, lon), F32)
        cross = jnp.zeros((8, lon), F32)
        for row in range(lat):
            own_cells = rows[row][:, :lon]
            upper_ref[row, group, :] = own_cells
            square = square + own_cells * own_cells
            if second:
                cross = cross + own_cells * before_ref[row, group, :]
        dots_ref[0, group, :] = square
        if second:
            dots_ref[1, group, :] = cross
        rows = spread_steps(rows, coefs)
        for row in range(lat):
            low_field = rows[row][:, :lon] * sigma_ref[row, :][None, :]
            lower_ref[row, group, :] = low_field

    for row in range(lat):
        high, low = split(lower_ref[row])
        halves[pl.ds(0, members), pl.ds(row * lon, lon)] = high
        halves[pl.ds(members, members), pl.ds(row * lon, lon)] = low
    sums[...] = jnp.zeros_like(sums)
    contract = (((1,), (1,)), ((), ()))
    for side, tile_ref in enumerate((own_ref, other_ref)):
        for slot in range(0, slots, 2):
            both = lax.dot_general(
                halves[...], tile_ref[pl.ds(slot * obs, 2 * obs), :], contract, preferred_element_type=F32
            )
            total = both[:members] + both[members:]
            for k in range(2):
                target = target_ref[side, slot + k]
                place = (target // 2) * count + side * 2 + target % 2
                sums[place] = sums[place] + total[:, k * obs : (k + 1) * obs] * live_ref[side, slot + k]
    for offset in range(OFFSETS):
        pieces[offset][...] = sums[pl.ds(offset * count, count)]


def forward(field, first, last, steps, sigma, own, other, targets, live, count, edge, before=None):
    lat, members, lon = field.shape
    obs = own.shape[0] // targets.shape[1]
    more = () if before is None else (before,)
    shape = jax.ShapeDtypeStruct((lat, members, lon), F32)
    piece = jax.ShapeDtypeStruct((count, members, obs), F32)
    dots = jax.ShapeDtypeStruct((1 + len(more), members, lon), F32)
    return pl.pallas_call(
        functools.partial(forward_kernel, edge, before is not None),
        out_shape=(shape, shape, dots) + (piece,) * OFFSETS,
        in_specs=[smem(), smem()] + [vmem()] * (7 + len(more)),
        out_specs=(vmem(),) * (3 + OFFSETS),
        scratch_shapes=[
            pltpu.VMEM((2 * members, lat * lon), BF16),
            pltpu.VMEM((OFFSETS * count, members, obs), F32),
        ],
        compiler_params=kernel_params(),
        cost_estimate=pl.CostEstimate(
            flops=8 * members * own.size, bytes_accessed=4 * own.size, transcendentals=0
        ),
        name="forward",
    )(targets, live, field, first, last, steps, sigma, own, other, *more)


def finish_kernel(edge, field_ref, first_ref, last_ref, steps_ref, dots_ref, *refs):
    start_ref, image_ref, start_low_ref, image_low_ref, increment_ref, residual_ref = refs
    lat, members, lon = field_ref.shape

    @pl.loop(0, members // 8)
    def _(index):
        group = pl.ds(pl.multiple_of(index * 8, 8), 8)
        coefs = coefficients(steps_ref, group)
        rows = extended_rows(field_ref, first_ref, last_ref, edge, group)
        rows = spread_steps(rows, coefs)
        pp, pg, gg, gh = [dots_ref[group, pl.ds(k, 1)] for k in range(4)]
        step0 = pp / (pp + pg)
        u, w = 1.0 - step0, -step0
        norm1 = u * u * pp + 2.0 * u * w * pg + w * w * gg
        x = u + norm1 / pp
        curve = x * (x * pp + (x + w) * pg + w * gg) + w * (x * pg + (x + w) * gg + w * gh)
        step1 = norm1 / curve
        inc_p, inc_g = step0 + step1 * x, step1 * w
        res_p, res_g, res_h = u - step1 * x, w - step1 * (x + w), -step1 * w
        for row in range(lat):
            increment_ref[group, row, :] = (
                inc_p * start_low_ref[row, group, :] + inc_g * image_low_ref[row, group, :]
            )
            residual_ref[group, row, :] = (
                res_p * start_ref[row, group, :]
                + res_g * image_ref[row, group, :]
                + res_h * rows[row][:, :lon]
            )


def finish(field, first, last, steps, dots, start, image, start_low, image_low, edge):
    lat, members, lon = field.shape
    out = jax.ShapeDtypeStruct((members, lat, lon), F32)
    return pl.pallas_call(
        functools.partial(finish_kernel, edge),
        out_shape=(out, out),
        in_specs=[vmem()] * 9,
        out_specs=(vmem(), vmem()),
        compiler_params=kernel_params(),
        name="finish",
    )(field, first, last, steps, dots, start, image, start_low, image_low)


def local(footprints, slot_target, slot_count, step_count, sigma, innovations, obs_weight):
    tiles = footprints[0, 0]
    slots, obs, lat, lon = tiles.shape
    blocks, ensemble, _ = innovations.shape
    members = step_count.shape[0]
    mine = lax.axis_index("obs")
    steps = step_count[:, None]
    live = (jnp.arange(slots, dtype=jnp.int32) < slot_count[0, 0]).astype(F32)
    weighted = (obs_weight[:, None, :] * innovations).astype(BF16).astype(F32)
    kept = lax.dynamic_slice_in_dim(weighted, mine * members, members, 1)
    given = lax.dynamic_slice_in_dim(weighted, (1 - mine) * members, members, 1)
    facts = jnp.concatenate([slot_target[0, 0].astype(F32), live, jnp.zeros((obs - 2 * slots,), F32)])
    packet = jnp.concatenate([given.reshape(-1, obs), obs_weight, facts[None]])
    got = shifted(packet, "obs", 1)
    rows = blocks * members
    given = got[:rows].reshape(blocks, members, obs)
    weight = jnp.concatenate([obs_weight, got[rows : rows + blocks]])
    facts = jnp.stack([facts, got[rows + blocks]])
    targets = facts[:, :slots].astype(jnp.int32)
    live = facts[:, slots : 2 * slots]
    start_blocks = jnp.concatenate([kept, given]).astype(BF16)
    count = 2 * blocks

    other_tiles = shifted(tiles, "obs", 1)
    tiles, got = lax.optimization_barrier((tiles, got))
    own = flatten_tiles(tiles)
    other = flatten_tiles(other_tiles)

    def nearby(block):
        return [block if k == REACH else shifted(block, "flux", REACH - k) for k in range(OFFSETS)]

    def back(pieces, edge):
        return adjoint(pieces, targets, live, own, other, sigma, count, members, edge)

    def home(pieces):
        total = pieces[REACH]
        for k in range(OFFSETS):
            if k != REACH:
                total = total + shifted(pieces[k], "flux", k - REACH)
        return total

    def ahead(field, first, last, *before):
        first, last = shifted(first, "flux", -1), shifted(last, "flux", 1)
        return forward(
            field, first, last, steps, sigma, own, other, targets, live, count, wide, *before
        )

    def weigh(values):
        return (weight[:, None, :] * values).reshape(-1, obs)

    wide = 2 * KMAX
    start, start_low, dots, *pieces = ahead(*back(nearby(start_blocks.reshape(-1, obs)), wide))
    pp = jnp.sum(dots[0], axis=1)
    image, image_low, dots, *pieces = ahead(*back(nearby(weigh(home(pieces))), wide), start)
    gg, pg = jnp.sum(dots[0], axis=1), jnp.sum(dots[1], axis=1)
    total = home(pieces)
    weighted = weigh(total)
    gh = jnp.sum(total * weighted.reshape(total.shape), axis=(0, 2))
    products = jnp.stack([pp, pg, gg, gh])
    if lax.axis_size("flux") == 8:
        size = products.size
        flat = products.reshape(1, size)
        tail = jnp.pad(flat, ((0, 7), (0, obs - size)))
        pieces = nearby(jnp.concatenate([weighted, tail]))
        across = shifted(tail, "flux", 4)
        rows = count * members
        tails = [piece[rows : rows + 8] for piece in pieces]
        field, first, last = back(pieces, KMAX)
        cells = first.shape[1]
        first, last = [
            shifted(jnp.concatenate([jnp.pad(part, ((0, 0), (0, obs - cells))), far]), "flux", way)
            for part, far, way in ((first, tails[-1], -1), (last, tails[0], 1))
        ]
        tails = tails + [across, first[members:], last[members:]]
        products = functools.reduce(jnp.add, tails)[0, :size].reshape(products.shape)
        first, last = first[:members, :cells], last[:members, :cells]
    else:
        products = lax.psum(products, "flux")
        field, first, last = back(nearby(weighted), KMAX)
        first, last = shifted(first, "flux", -1), shifted(last, "flux", 1)
    return finish(field, first, last, steps, products.T, start, image, start_low, image_low, KMAX)


def solution(mesh):
    return jax.shard_map(
        local,
        mesh=mesh,
        in_specs=(
            P(("group", "flux"), "obs", None, None, None, None),
            P(("group", "flux"), "obs", None),
            P(("group", "flux"), "obs"),
            P(("group", "obs")),
            P("group", "flux"),
            P(("group", "flux", "obs"), None, None),
            P(("group", "flux", "obs"), None),
        ),
        out_specs=(P(("group", "obs"), None, "flux"), P(("group", "obs"), None, "flux")),
        check_vma=False,
    )
```

```python
import functools

import jax
import jax.numpy as jnp
from jax import lax
from jax.experimental import pallas as pl
from jax.experimental.pallas import tpu as pltpu
from jax.sharding import PartitionSpec as P

REACH = 2
KMAX = 4
OFFSETS = 2 * REACH + 1
SPREAD = 0.24
F32 = jnp.float32
BF16 = jnp.bfloat16
VMEM_LIMIT = 16 * 1024 * 1024
STRIDE = 3


def shifted(block, axis, distance):
    size = lax.axis_size(axis)
    return lax.ppermute(block, axis, [(i, (i + distance) % size) for i in range(size)])


def kernel_params(**more):
    return pltpu.CompilerParams(vmem_limit_bytes=VMEM_LIMIT, **more)


def vmem():
    return pl.BlockSpec(memory_space=pltpu.VMEM)


def smem():
    return pl.BlockSpec(memory_space=pltpu.SMEM)


def flatten_kernel(pitch, tile_ref, out_ref, held, wide, sems):
    slots, obs, lat, lon = tile_ref.shape
    copies = [
        pltpu.make_async_copy(tile_ref.at[slot], held.at[slot], sems.at[slot]) for slot in range(slots)
    ]
    for copy in copies:
        copy.start()
    for slot, copy in enumerate(copies):
        copy.wait()
        for start in range(0, obs, 16):
            side = start // 16 % 2
            for k in range(16):
                wide[side, pl.ds(k * pitch, lat, stride=STRIDE), :] = held[slot, start + k].astype(F32)
            for row in range(lat):
                part = wide[side, pl.ds(row * STRIDE, 16, stride=pitch), :]
                out_ref[pl.ds(slot * obs + start, 16), pl.ds(row * lon, lon)] = part.astype(BF16)


def flatten_tiles(tiles):
    slots, obs, lat, lon = tiles.shape
    pitch = (lat * STRIDE) | 1
    return pl.pallas_call(
        functools.partial(flatten_kernel, pitch),
        out_shape=jax.ShapeDtypeStruct((slots * obs, lat * lon), BF16),
        in_specs=[pl.BlockSpec(memory_space=pltpu.HBM)],
        out_specs=vmem(),
        scratch_shapes=[
            pltpu.VMEM(tiles.shape, BF16),
            pltpu.VMEM((2, 16 * pitch, lon), F32),
            pltpu.SemaphoreType.DMA((slots,)),
        ],
        compiler_params=kernel_params(),
        cost_estimate=pl.CostEstimate(flops=0, bytes_accessed=4 * tiles.size, transcendentals=0),
        name="flatten_tiles",
    )(tiles)


def prepare_kernel(mine_ref, target_ref, count_ref, innovation_ref, weight_ref, steps_ref, *outs):
    packet_ref, kept_ref, table_ref = outs
    blocks, _, obs = innovation_ref.shape
    members = table_ref.shape[0]
    slots = target_ref.shape[0]
    mine = mine_ref[0]
    for block in range(blocks):
        rows = pl.ds(block * members, members)
        halves = [
            (weight_ref[pl.ds(block, 1), :] * innovation_ref[block, pl.ds(k * members, members), :])
            .astype(BF16)
            .astype(F32)
            for k in range(2)
        ]
        kept_ref[rows, :] = jnp.where(mine == 0, halves[0], halves[1])
        packet_ref[rows, :] = jnp.where(mine == 0, halves[1], halves[0])
    lane = lax.broadcasted_iota(jnp.int32, (1, obs), 1)
    facts = jnp.zeros((1, obs), F32)
    for slot in range(slots):
        facts = jnp.where(lane == slot, target_ref[slot].astype(F32), facts)
        alive = jnp.where(slot < count_ref[0], 1.0, 0.0)
        facts = jnp.where(lane == slots + slot, alive, facts)
    base = blocks * members
    packet_ref[pl.ds(base, 8), :] = jnp.concatenate(
        [weight_ref[...], facts, jnp.zeros((8 - blocks - 1, obs), F32)], axis=0
    )
    table_ref[...] = jnp.broadcast_to(steps_ref[...].astype(F32), table_ref.shape)


def prepare(mine, targets, count, innovations, weight, steps):
    blocks, _, obs = innovations.shape
    members = steps.shape[0]
    return pl.pallas_call(
        prepare_kernel,
        out_shape=(
            jax.ShapeDtypeStruct((blocks * members + 8, obs), F32),
            jax.ShapeDtypeStruct((blocks * members, obs), F32),
            jax.ShapeDtypeStruct((members, obs), F32),
        ),
        in_specs=[smem()] * 3 + [vmem()] * 3,
        out_specs=(vmem(),) * 3,
        compiler_params=kernel_params(),
        name="prepare",
    )(mine, targets, count, innovations, weight, steps)


def split(value):
    high = value.astype(BF16)
    return high, (value - high.astype(F32)).astype(BF16)


def adjoint_kernel(edge, carry, target_ref, live_ref, *refs):
    pieces = refs[:OFFSETS]
    own_ref, other_ref, sigma_ref, field_ref, first_ref, last_ref, near, picked = refs[OFFSETS:]
    members = picked.shape[0] // 2
    obs = pieces[0].shape[1]
    rows = near.shape[0] // OFFSETS
    count = rows // members
    slots = own_ref.shape[0] // obs
    lat, lon = sigma_ref.shape
    for offset in range(OFFSETS):
        near[pl.ds(offset * rows, rows), :] = pieces[offset][pl.ds(0, rows), :].astype(F32)
    for side in range(2):
        for slot in range(slots):
            target = target_ref[side, slot]
            place = (target // 2) * count + side * 2 + target % 2
            block = near[pl.ds(pl.multiple_of(place * members, members), members), :] * live_ref[side, slot]
            high, low = split(block)
            columns = pl.ds((side * slots + slot) * obs, obs)
            picked[pl.ds(0, members), columns] = high
            picked[pl.ds(members, members), columns] = low
    if carry:
        first_ref[pl.ds(members, 8), :] = pieces[-1][pl.ds(rows, 8), :]
        last_ref[pl.ds(members, 8), :] = pieces[0][pl.ds(rows, 8), :]
    half = slots * obs
    for row in range(0, lat, 2):
        cells = pl.ds(row * lon, 2 * lon)
        both = jnp.dot(picked[:, :half], own_ref[:, cells], preferred_element_type=F32)
        both = both + jnp.dot(picked[:, half:], other_ref[:, cells], preferred_element_type=F32)
        total = both[:members] + both[members:]
        for k in range(2):
            field = total[:, k * lon : (k + 1) * lon] * sigma_ref[row + k, :][None, :]
            field_ref[row + k] = field
            span = pl.ds((row + k) * edge, edge)
            first_ref[pl.ds(0, members), span] = field[:, :edge]
            last_ref[pl.ds(0, members), span] = field[:, lon - edge :]


def adjoint(pieces, targets, live, own, other, sigma, count, members, edge):
    obs = pieces[0].shape[1]
    lat, lon = sigma.shape
    carry = pieces[0].shape[0] > count * members
    edges = jax.ShapeDtypeStruct((members + 8 * carry, max(lat * edge, obs)), F32)
    return pl.pallas_call(
        functools.partial(adjoint_kernel, edge, carry),
        out_shape=(
            jax.ShapeDtypeStruct((lat, members, lon), F32),
            edges,
            edges,
        ),
        in_specs=[smem(), smem()] + [vmem()] * (OFFSETS + 3),
        out_specs=(vmem(), vmem(), vmem()),
        scratch_shapes=[
            pltpu.VMEM((OFFSETS * count * members, obs), F32),
            pltpu.VMEM((2 * members, 2 * own.shape[0]), BF16),
        ],
        compiler_params=kernel_params(),
        cost_estimate=pl.CostEstimate(
            flops=8 * members * own.size, bytes_accessed=4 * own.size, transcendentals=0
        ),
        name="adjoint",
    )(targets, live, *pieces, own, other, sigma)


def spread_steps(rows, coefs):
    zero = jnp.zeros_like(rows[0])
    lanes = rows[0].shape[1]
    for coef in coefs:
        keep = 1.0 - 4.0 * coef
        padded = [zero] + rows + [zero]
        rows = [
            keep * padded[i]
            + coef
            * (
                (padded[i - 1] + padded[i + 1])
                + (pltpu.roll(padded[i], 1, 1) + pltpu.roll(padded[i], lanes - 1, 1))
            )
            for i in range(1, len(rows) + 1)
        ]
    return rows


def extended_rows(field_ref, first_ref, last_ref, edge, group):
    lat, _, lon = field_ref.shape
    rows = []
    for row in range(lat):
        after = first_ref[group, pl.ds(row * edge, edge)]
        before = last_ref[group, pl.ds(row * edge, edge)]
        gap = jnp.zeros((8, lon - 2 * edge), F32)
        rows.append(jnp.concatenate([field_ref[row, group, :], after, gap, before], axis=1))
    return rows


def coefficients(steps_ref, group):
    steps = steps_ref[group, pl.ds(0, 1)]
    return [jnp.where(steps > step + 0.5, SPREAD, 0.0).astype(F32) for step in range(KMAX)]


def forward_kernel(edge, second, target_ref, live_ref, *refs):
    field_ref, first_ref, last_ref, steps_ref, sigma_ref, own_ref, other_ref = refs[:7]
    refs = refs[7:]
    if second:
        before_ref, refs = refs[0], refs[1:]
    upper_ref, lower_ref, dots_ref = refs[:3]
    pieces = refs[3 : 3 + OFFSETS]
    halves, sums = refs[3 + OFFSETS :]
    lat, members, lon = field_ref.shape
    obs = sums.shape[2]
    slots = own_ref.shape[0] // obs
    count = pieces[0].shape[0]

    @pl.loop(0, members // 8)
    def _(index):
        group = pl.ds(pl.multiple_of(index * 8, 8), 8)
        coefs = coefficients(steps_ref, group)
        rows = extended_rows(field_ref, first_ref, last_ref, edge, group)
        rows = spread_steps(rows, coefs)
        square = jnp.zeros((8, lon), F32)
        cross = jnp.zeros((8, lon), F32)
        for row in range(lat):
            own_cells = rows[row][:, :lon]
            upper_ref[row, group, :] = own_cells
            square = square + own_cells * own_cells
            if second:
                cross = cross + own_cells * before_ref[row, group, :]
        dots_ref[0, group, :] = square
        if second:
            dots_ref[1, group, :] = cross
        rows = spread_steps(rows, coefs)
        for row in range(lat):
            low_field = rows[row][:, :lon] * sigma_ref[row, :][None, :]
            lower_ref[row, group, :] = low_field

    for row in range(lat):
        high, low = split(lower_ref[row])
        halves[pl.ds(0, members), pl.ds(row * lon, lon)] = high
        halves[pl.ds(members, members), pl.ds(row * lon, lon)] = low
    sums[...] = jnp.zeros_like(sums)
    contract = (((1,), (1,)), ((), ()))
    for side, tile_ref in enumerate((own_ref, other_ref)):
        for slot in range(0, slots, 2):
            both = lax.dot_general(
                halves[...], tile_ref[pl.ds(slot * obs, 2 * obs), :], contract, preferred_element_type=F32
            )
            total = both[:members] + both[members:]
            for k in range(2):
                target = target_ref[side, slot + k]
                place = (target // 2) * count + side * 2 + target % 2
                sums[place] = sums[place] + total[:, k * obs : (k + 1) * obs] * live_ref[side, slot + k]
    for offset in range(OFFSETS):
        pieces[offset][...] = sums[pl.ds(offset * count, count)]


def forward(field, first, last, steps, sigma, own, other, targets, live, count, edge, before=None):
    lat, members, lon = field.shape
    obs = own.shape[0] // targets.shape[1]
    more = () if before is None else (before,)
    shape = jax.ShapeDtypeStruct((lat, members, lon), F32)
    piece = jax.ShapeDtypeStruct((count, members, obs), F32)
    dots = jax.ShapeDtypeStruct((1 + len(more), members, lon), F32)
    return pl.pallas_call(
        functools.partial(forward_kernel, edge, before is not None),
        out_shape=(shape, shape, dots) + (piece,) * OFFSETS,
        in_specs=[smem(), smem()] + [vmem()] * (7 + len(more)),
        out_specs=(vmem(),) * (3 + OFFSETS),
        scratch_shapes=[
            pltpu.VMEM((2 * members, lat * lon), BF16),
            pltpu.VMEM((OFFSETS * count, members, obs), F32),
        ],
        compiler_params=kernel_params(),
        cost_estimate=pl.CostEstimate(
            flops=8 * members * own.size, bytes_accessed=4 * own.size, transcendentals=0
        ),
        name="forward",
    )(targets, live, field, first, last, steps, sigma, own, other, *more)


def weigh_kernel(*refs):
    pieces = refs[:OFFSETS]
    weight_ref, first_ref, second_ref, out_ref = refs[OFFSETS:]
    count, members, obs = pieces[0].shape
    curve = jnp.zeros((members, obs), F32)
    for block in range(count):
        total = pieces[0][block]
        for piece in pieces[1:]:
            total = total + piece[block]
        weighted = total * weight_ref[pl.ds(block, 1), :]
        curve = curve + total * weighted
        out_ref[pl.ds(block * members, members), :] = weighted
    parts = jnp.concatenate([first_ref[0], second_ref[1], second_ref[0], curve], axis=0)
    out_ref[pl.ds(count * members, 8), :] = lax.dot_general(
        jnp.ones((8, obs), F32),
        parts,
        (((1,), (1,)), ((), ())),
        precision=lax.Precision.HIGHEST,
        preferred_element_type=F32,
    )


def weigh(pieces, weight, first, second):
    count, members, obs = pieces[0].shape
    return pl.pallas_call(
        weigh_kernel,
        out_shape=jax.ShapeDtypeStruct((count * members + 8, obs), F32),
        in_specs=[vmem()] * (OFFSETS + 3),
        out_specs=vmem(),
        compiler_params=kernel_params(),
        name="weigh",
    )(*pieces, weight, first, second)


def finish_kernel(edge, starts, field_ref, first_ref, last_ref, steps_ref, *refs):
    tails, refs = refs[: len(starts)], refs[len(starts) :]
    start_ref, image_ref, start_low_ref, image_low_ref, increment_ref, residual_ref, dots = refs
    lat, members, lon = field_ref.shape
    row = jnp.zeros((8, dots.shape[0]), F32)
    for tail, begin in zip(tails, starts):
        row = row + tail[pl.ds(begin, 8), :]
    square = (dots.shape[0], dots.shape[0])
    diagonal = lax.broadcasted_iota(jnp.int32, square, 0) == lax.broadcasted_iota(jnp.int32, square, 1)
    dots[...] = jnp.sum(jnp.where(diagonal, row[0:1], 0.0), axis=1, keepdims=True)

    @pl.loop(0, members // 8)
    def _(index):
        begin = pl.multiple_of(index * 8, 8)
        group = pl.ds(begin, 8)
        coefs = coefficients(steps_ref, group)
        rows = extended_rows(field_ref, first_ref, last_ref, edge, group)
        rows = spread_steps(rows, coefs)
        pp, pg, gg, gh = [dots[pl.ds(begin + k * members, 8), :] for k in range(4)]
        step0 = pp / (pp + pg)
        u, w = 1.0 - step0, -step0
        norm1 = u * u * pp + 2.0 * u * w * pg + w * w * gg
        x = u + norm1 / pp
        curve = x * (x * pp + (x + w) * pg + w * gg) + w * (x * pg + (x + w) * gg + w * gh)
        step1 = norm1 / curve
        inc_p, inc_g = step0 + step1 * x, step1 * w
        res_p, res_g, res_h = u - step1 * x, w - step1 * (x + w), -step1 * w
        for row in range(lat):
            increment_ref[group, row, :] = (
                inc_p * start_low_ref[row, group, :] + inc_g * image_low_ref[row, group, :]
            )
            residual_ref[group, row, :] = (
                res_p * start_ref[row, group, :]
                + res_g * image_ref[row, group, :]
                + res_h * rows[row][:, :lon]
            )


def finish(field, first, last, steps, tails, start, image, start_low, image_low, edge):
    lat, members, lon = field.shape
    out = jax.ShapeDtypeStruct((members, lat, lon), F32)
    starts = [begin for _, begin in tails]
    return pl.pallas_call(
        functools.partial(finish_kernel, edge, starts),
        out_shape=(out, out),
        in_specs=[vmem()] * (8 + len(tails)),
        out_specs=(vmem(), vmem()),
        scratch_shapes=[pltpu.VMEM((4 * members, 1), F32)],
        compiler_params=kernel_params(),
        name="finish",
    )(field, first, last, steps, *[part for part, _ in tails], start, image, start_low, image_low)


def local(footprints, slot_target, slot_count, step_count, sigma, innovations, obs_weight):
    tiles = footprints[0, 0]
    slots, obs, lat, lon = tiles.shape
    blocks = innovations.shape[0]
    members = step_count.shape[0]
    count = 2 * blocks
    mine = lax.axis_index("obs").astype(jnp.int32).reshape(1)
    packet, kept, steps = prepare(
        mine, slot_target[0, 0], slot_count[0], innovations, obs_weight, step_count[:, None]
    )
    got = shifted(packet, "obs", 1)
    base = blocks * members
    weight = jnp.concatenate([obs_weight, got[base : base + blocks]])
    facts = jnp.stack([packet[base + blocks], got[base + blocks]])
    targets = facts[:, :slots].astype(jnp.int32)
    live = facts[:, slots : 2 * slots]
    start_blocks = jnp.concatenate([kept, got[:base]]).astype(BF16)

    other_tiles = shifted(tiles, "obs", 1)
    tiles, got = lax.optimization_barrier((tiles, got))
    own = flatten_tiles(tiles)
    other = flatten_tiles(other_tiles)

    def nearby(block):
        return [block if k == REACH else shifted(block, "flux", REACH - k) for k in range(OFFSETS)]

    def back(pieces, edge):
        field, first, last = adjoint(
            pieces, targets, live, own, other, sigma, count, members, edge
        )
        return field, shifted(first, "flux", -1), shifted(last, "flux", 1)

    def home(pieces):
        return [
            piece if k == REACH else shifted(piece, "flux", k - REACH) for k, piece in enumerate(pieces)
        ]

    def ahead(field, first, last, *before):
        return forward(
            field, first, last, steps, sigma, own, other, targets, live, count, wide, *before
        )

    wide = 2 * KMAX
    start, start_low, first_dots, *pieces = ahead(*back(nearby(start_blocks), wide))
    total = functools.reduce(jnp.add, home(pieces))
    image, image_low, dots, *pieces = ahead(
        *back(nearby((weight[:, None, :] * total).reshape(-1, obs)), wide), start
    )
    weighted = weigh(home(pieces), weight, first_dots, dots)
    rows = count * members
    if lax.axis_size("flux") == 8:
        pieces = nearby(weighted)
        across = shifted(weighted[rows:], "flux", 4)
        field, first, last = back(pieces, KMAX)
        tails = [(piece, rows) for piece in pieces] + [(across, 0), (first, members), (last, members)]
    else:
        tails = [(lax.psum(weighted[rows:], "flux"), 0)]
        field, first, last = back(nearby(weighted[:rows]), KMAX)
    return finish(field, first, last, steps, tails, start, image, start_low, image_low, KMAX)


def solution(mesh):
    return jax.shard_map(
        local,
        mesh=mesh,
        in_specs=(
            P(("group", "flux"), "obs", None, None, None, None),
            P(("group", "flux"), "obs", None),
            P(("group", "flux"), "obs"),
            P(("group", "obs")),
            P("group", "flux"),
            P(("group", "flux", "obs"), None, None),
            P(("group", "flux", "obs"), None),
        ),
        out_specs=(P(("group", "obs"), None, "flux"), P(("group", "obs"), None, "flux")),
        check_vma=False,
    )
```

```python
import functools

import jax
import jax.numpy as jnp
from jax import lax
from jax.experimental import pallas as pl
from jax.experimental.pallas import tpu as pltpu
from jax.sharding import PartitionSpec as P

REACH = 2
KMAX = 4
OFFSETS = 2 * REACH + 1
SPREAD = 0.24
F32 = jnp.float32
BF16 = jnp.bfloat16
VMEM_LIMIT = 16 * 1024 * 1024
STRIDE = 3
EXTRA = 16
TOP = 250.0
MIDDLE = 125.0


def shifted(block, axis, distance):
    size = lax.axis_size(axis)
    return lax.ppermute(block, axis, [(i, (i + distance) % size) for i in range(size)])


def kernel_params(**more):
    return pltpu.CompilerParams(vmem_limit_bytes=VMEM_LIMIT, **more)


def vmem():
    return pl.BlockSpec(memory_space=pltpu.VMEM)


def smem():
    return pl.BlockSpec(memory_space=pltpu.SMEM)


def flatten_kernel(pitch, tile_ref, out_ref, held, wide, sems):
    slots, obs, lat, lon = tile_ref.shape
    copies = [
        pltpu.make_async_copy(tile_ref.at[slot], held.at[slot], sems.at[slot]) for slot in range(slots)
    ]
    for copy in copies:
        copy.start()
    for slot, copy in enumerate(copies):
        copy.wait()
        for start in range(0, obs, 16):
            side = start // 16 % 2
            for k in range(16):
                wide[side, pl.ds(k * pitch, lat, stride=STRIDE), :] = held[slot, start + k].astype(F32)
            for row in range(lat):
                part = wide[side, pl.ds(row * STRIDE, 16, stride=pitch), :]
                out_ref[pl.ds(slot * obs + start, 16), pl.ds(row * lon, lon)] = part.astype(BF16)


def flatten_tiles(tiles):
    slots, obs, lat, lon = tiles.shape
    pitch = (lat * STRIDE) | 1
    return pl.pallas_call(
        functools.partial(flatten_kernel, pitch),
        out_shape=jax.ShapeDtypeStruct((slots * obs, lat * lon), BF16),
        in_specs=[pl.BlockSpec(memory_space=pltpu.HBM)],
        out_specs=vmem(),
        scratch_shapes=[
            pltpu.VMEM(tiles.shape, BF16),
            pltpu.VMEM((2, 16 * pitch, lon), F32),
            pltpu.SemaphoreType.DMA((slots,)),
        ],
        compiler_params=kernel_params(),
        cost_estimate=pl.CostEstimate(flops=0, bytes_accessed=4 * tiles.size, transcendentals=0),
        name="flatten_tiles",
    )(tiles)


def prepare_kernel(mine_ref, count_ref, *refs):
    sources, outs, held, sems = refs[:4], refs[4:7], refs[7:11], refs[11]
    packet_ref, kept_ref, table_ref = outs
    target_ref, steps_ref, innovation_ref, weight_ref = held
    blocks, _, obs = innovation_ref.shape
    members = table_ref.shape[0]
    slots = target_ref.shape[2]
    copies = [pltpu.make_async_copy(a, b, sems.at[k]) for k, (a, b) in enumerate(zip(sources, held))]
    for copy in copies:
        copy.start()
    for copy in copies:
        copy.wait()
    for member in range(members):
        table_ref[pl.ds(member, 1), :] = jnp.full((1, obs), steps_ref[member].astype(F32))
    lane = lax.broadcasted_iota(jnp.int32, (1, obs), 1)
    facts = jnp.zeros((1, obs), F32)
    for slot in range(slots):
        facts = jnp.where(lane == slot, target_ref[0, 0, slot].astype(F32), facts)
        alive = jnp.where(slot < count_ref[0, 0], 1.0, 0.0)
        facts = jnp.where(lane == slots + slot, alive, facts)
    mine = mine_ref[0]
    for block in range(blocks):
        rows = pl.ds(block * members, members)
        halves = [
            (weight_ref[pl.ds(block, 1), :] * innovation_ref[block, pl.ds(k * members, members), :])
            .astype(BF16)
            .astype(F32)
            for k in range(2)
        ]
        kept_ref[rows, :] = jnp.where(mine == 0, halves[0], halves[1])
        packet_ref[rows, :] = jnp.where(mine == 0, halves[1], halves[0])
    base = blocks * members
    packet_ref[pl.ds(base, 8), :] = jnp.concatenate(
        [weight_ref[...], facts, jnp.zeros((8 - blocks - 1, obs), F32)], axis=0
    )


def in_hbm(value):
    return pltpu.with_memory_space_constraint(value, pltpu.HBM)


def prepare(mine, targets, count, steps, innovations, weight):
    blocks, _, obs = innovations.shape
    members = steps.shape[0]
    sources = (targets, steps, innovations, weight)
    spaces = (pltpu.SMEM, pltpu.SMEM, pltpu.VMEM, pltpu.VMEM)
    return pl.pallas_call(
        prepare_kernel,
        out_shape=(
            jax.ShapeDtypeStruct((blocks * members + 8, obs), F32),
            jax.ShapeDtypeStruct((blocks * members, obs), F32),
            jax.ShapeDtypeStruct((members, obs), F32),
        ),
        in_specs=[smem()] * 2 + [pl.BlockSpec(memory_space=pltpu.HBM)] * len(sources),
        out_specs=(vmem(),) * 3,
        scratch_shapes=[space(part.shape, part.dtype) for space, part in zip(spaces, sources)]
        + [pltpu.SemaphoreType.DMA((len(sources),))],
        compiler_params=kernel_params(),
        name="prepare",
    )(mine, count, *[in_hbm(part) for part in sources])


def split(value):
    high = value.astype(BF16)
    return high, (value - high.astype(F32)).astype(BF16)


def thirds(row):
    parts = []
    for _ in range(3):
        part = row.astype(BF16).astype(F32)
        parts.append(part)
        row = row - part
    return parts


def encode(value, scale):
    level = jnp.abs(value) * (TOP / scale)
    whole = jnp.floor(level)
    code = (1.0 + level - whole) * jnp.exp2(whole - MIDDLE)
    return jnp.where(value < 0.0, -code, code).astype(BF16)


def decode(code, unit):
    code = code.astype(F32)
    size = jnp.abs(code)
    whole = jnp.floor(jnp.log2(size))
    value = (whole + (MIDDLE - 1.0) + size * jnp.exp2(-whole)) * unit
    return jnp.where(code < 0.0, -value, value)


def largest(values):
    top = jnp.max(jnp.abs(values), axis=0, keepdims=True)
    return jnp.maximum(jnp.max(top, axis=1, keepdims=True), 1e-30)


def encode_piece(out_ref, values, carried=None):
    rows, lanes = values.shape
    scale = largest(values)
    out_ref[pl.ds(0, rows), :] = encode(values, scale)
    zero = jnp.zeros((1, lanes), F32)
    lines = thirds(jnp.broadcast_to(scale, (1, lanes))) + [zero] * 5
    lines = lines + (thirds(carried) + [zero] * 5 if carried is not None else [zero] * 8)
    out_ref[pl.ds(rows, EXTRA), :] = jnp.concatenate(lines, axis=0).astype(BF16)


def carried_row(ref, rows, begin):
    lines = ref[pl.ds(rows, EXTRA), :].astype(F32)
    return lines[begin : begin + 1] + lines[begin + 1 : begin + 2] + lines[begin + 2 : begin + 3]


def decode_piece(ref, rows):
    unit = carried_row(ref, rows, 0) * (1.0 / TOP)
    return decode(ref[pl.ds(0, rows), :], unit)


def adjoint_kernel(edge, coded, carry, target_ref, live_ref, *refs):
    pieces = refs[:OFFSETS]
    own_ref, other_ref, sigma_ref, field_ref, first_ref, last_ref, near, picked = refs[OFFSETS:]
    members = picked.shape[0] // 2
    obs = pieces[0].shape[1]
    rows = near.shape[0] // OFFSETS
    count = rows // members
    slots = own_ref.shape[0] // obs
    lat, lon = sigma_ref.shape
    for offset in range(OFFSETS):
        if coded and offset != REACH:
            block = decode_piece(pieces[offset], rows)
        else:
            block = pieces[offset][...].astype(F32)
        near[pl.ds(offset * rows, rows), :] = block
    for side in range(2):
        for slot in range(slots):
            target = target_ref[side, slot]
            place = (target // 2) * count + side * 2 + target % 2
            block = near[pl.ds(pl.multiple_of(place * members, members), members), :] * live_ref[side, slot]
            high, low = split(block)
            columns = pl.ds((side * slots + slot) * obs, obs)
            picked[pl.ds(0, members), columns] = high
            picked[pl.ds(members, members), columns] = low
    if carry:
        first_ref[pl.ds(members, 8), :] = jnp.broadcast_to(carried_row(pieces[-1], rows, 8), (8, obs))
        last_ref[pl.ds(members, 8), :] = jnp.broadcast_to(carried_row(pieces[0], rows, 8), (8, obs))
    half = slots * obs
    for row in range(0, lat, 2):
        cells = pl.ds(row * lon, 2 * lon)
        both = jnp.dot(picked[:, :half], own_ref[:, cells], preferred_element_type=F32)
        both = both + jnp.dot(picked[:, half:], other_ref[:, cells], preferred_element_type=F32)
        total = both[:members] + both[members:]
        for k in range(2):
            field = total[:, k * lon : (k + 1) * lon] * sigma_ref[row + k, :][None, :]
            field_ref[row + k] = field
            span = pl.ds((row + k) * edge, edge)
            first_ref[pl.ds(0, members), span] = field[:, :edge]
            last_ref[pl.ds(0, members), span] = field[:, lon - edge :]


def adjoint(pieces, targets, live, own, other, sigma, count, members, edge, carry):
    obs = pieces[0].shape[1]
    lat, lon = sigma.shape
    coded = pieces[0].shape[0] > count * members
    edges = jax.ShapeDtypeStruct((members + 8 * carry, max(lat * edge, obs)), F32)
    return pl.pallas_call(
        functools.partial(adjoint_kernel, edge, coded, carry),
        out_shape=(
            jax.ShapeDtypeStruct((lat, members, lon), F32),
            edges,
            edges,
        ),
        in_specs=[smem(), smem()] + [vmem()] * (OFFSETS + 3),
        out_specs=(vmem(), vmem(), vmem()),
        scratch_shapes=[
            pltpu.VMEM((OFFSETS * count * members, obs), F32),
            pltpu.VMEM((2 * members, 2 * own.shape[0]), BF16),
        ],
        compiler_params=kernel_params(),
        cost_estimate=pl.CostEstimate(
            flops=8 * members * own.size, bytes_accessed=4 * own.size, transcendentals=0
        ),
        name="adjoint",
    )(targets, live, *pieces, own, other, sigma)


def spread_steps(rows, coefs):
    zero = jnp.zeros_like(rows[0])
    lanes = rows[0].shape[1]
    for coef in coefs:
        keep = 1.0 - 4.0 * coef
        padded = [zero] + rows + [zero]
        rows = [
            keep * padded[i]
            + coef
            * (
                (padded[i - 1] + padded[i + 1])
                + (pltpu.roll(padded[i], 1, 1) + pltpu.roll(padded[i], lanes - 1, 1))
            )
            for i in range(1, len(rows) + 1)
        ]
    return rows


def extended_rows(field_ref, first_ref, last_ref, edge, group):
    lat, _, lon = field_ref.shape
    rows = []
    for row in range(lat):
        after = first_ref[group, pl.ds(row * edge, edge)]
        before = last_ref[group, pl.ds(row * edge, edge)]
        gap = jnp.zeros((8, lon - 2 * edge), F32)
        rows.append(jnp.concatenate([field_ref[row, group, :], after, gap, before], axis=1))
    return rows


def coefficients(steps_ref, group):
    steps = steps_ref[group, pl.ds(0, 1)]
    return [jnp.where(steps > step + 0.5, SPREAD, 0.0).astype(F32) for step in range(KMAX)]


def forward_kernel(edge, second, target_ref, live_ref, *refs):
    field_ref, first_ref, last_ref, steps_ref, sigma_ref, own_ref, other_ref = refs[:7]
    refs = refs[7:]
    if second:
        before_ref, refs = refs[0], refs[1:]
    upper_ref, lower_ref, dots_ref = refs[:3]
    pieces = refs[3 : 3 + OFFSETS]
    halves, sums = refs[3 + OFFSETS :]
    lat, members, lon = field_ref.shape
    obs = sums.shape[1]
    slots = own_ref.shape[0] // obs
    rows = sums.shape[0] // OFFSETS
    count = rows // members

    @pl.loop(0, members // 8)
    def _(index):
        group = pl.ds(pl.multiple_of(index * 8, 8), 8)
        coefs = coefficients(steps_ref, group)
        rows = extended_rows(field_ref, first_ref, last_ref, edge, group)
        rows = spread_steps(rows, coefs)
        square = jnp.zeros((8, lon), F32)
        cross = jnp.zeros((8, lon), F32)
        for row in range(lat):
            own_cells = rows[row][:, :lon]
            upper_ref[row, group, :] = own_cells
            square = square + own_cells * own_cells
            if second:
                cross = cross + own_cells * before_ref[row, group, :]
        dots_ref[0, group, :] = square
        if second:
            dots_ref[1, group, :] = cross
        rows = spread_steps(rows, coefs)
        for row in range(lat):
            low_field = rows[row][:, :lon] * sigma_ref[row, :][None, :]
            lower_ref[row, group, :] = low_field

    for row in range(lat):
        high, low = split(lower_ref[row])
        halves[pl.ds(0, members), pl.ds(row * lon, lon)] = high
        halves[pl.ds(members, members), pl.ds(row * lon, lon)] = low
    sums[...] = jnp.zeros_like(sums)
    contract = (((1,), (1,)), ((), ()))
    for side, tile_ref in enumerate((own_ref, other_ref)):
        for slot in range(0, slots, 2):
            both = lax.dot_general(
                halves[...], tile_ref[pl.ds(slot * obs, 2 * obs), :], contract, preferred_element_type=F32
            )
            total = both[:members] + both[members:]
            for k in range(2):
                target = target_ref[side, slot + k]
                place = (target // 2) * count + side * 2 + target % 2
                block = pl.ds(pl.multiple_of(place * members, members), members)
                sums[block, :] = (
                    sums[block, :] + total[:, k * obs : (k + 1) * obs] * live_ref[side, slot + k]
                )
    for offset in range(OFFSETS):
        values = sums[pl.ds(offset * rows, rows), :]
        if offset == REACH:
            pieces[offset][...] = values
        else:
            encode_piece(pieces[offset], values)


def forward(field, first, last, steps, sigma, own, other, targets, live, count, edge, before=None):
    lat, members, lon = field.shape
    obs = own.shape[0] // targets.shape[1]
    more = () if before is None else (before,)
    shape = jax.ShapeDtypeStruct((lat, members, lon), F32)
    pieces = [jax.ShapeDtypeStruct((count * members + EXTRA, obs), BF16) for _ in range(OFFSETS)]
    pieces[REACH] = jax.ShapeDtypeStruct((count * members, obs), F32)
    dots = jax.ShapeDtypeStruct((1 + len(more), members, lon), F32)
    return pl.pallas_call(
        functools.partial(forward_kernel, edge, before is not None),
        out_shape=(shape, shape, dots, *pieces),
        in_specs=[smem(), smem()] + [vmem()] * (7 + len(more)),
        out_specs=(vmem(),) * (3 + OFFSETS),
        scratch_shapes=[
            pltpu.VMEM((2 * members, lat * lon), BF16),
            pltpu.VMEM((OFFSETS * count * members, obs), F32),
        ],
        compiler_params=kernel_params(),
        cost_estimate=pl.CostEstimate(
            flops=8 * members * own.size, bytes_accessed=4 * own.size, transcendentals=0
        ),
        name="forward",
    )(targets, live, field, first, last, steps, sigma, own, other, *more)


def weigh_kernel(*refs):
    pieces = refs[:OFFSETS]
    weight_ref, refs = refs[OFFSETS], refs[OFFSETS + 1 :]
    products = refs[:-3] if len(refs) > 3 else None
    coded_ref, plain_ref, row_ref = refs[-3:]
    count = weight_ref.shape[0]
    rows, obs = plain_ref.shape
    members = rows // count
    total = pieces[REACH][...]
    for offset in range(OFFSETS):
        if offset != REACH:
            total = total + decode_piece(pieces[offset], rows)
    weight = jnp.concatenate(
        [jnp.broadcast_to(weight_ref[pl.ds(block, 1), :], (members, obs)) for block in range(count)], axis=0
    )
    weighted = total * weight
    plain_ref[...] = weighted
    row_ref[...] = jnp.zeros_like(row_ref)
    row = None
    if products is not None:
        first_ref, second_ref = products
        curve = (total * weighted).reshape(count, members, obs)
        parts = jnp.concatenate(
            [first_ref[0], second_ref[1], second_ref[0], jnp.sum(curve, axis=0)], axis=0
        )
        row_ref[...] = lax.dot_general(
            jnp.ones((8, obs), F32),
            parts,
            (((1,), (1,)), ((), ())),
            precision=lax.Precision.HIGHEST,
            preferred_element_type=F32,
        )
        row = row_ref[pl.ds(0, 1), :]
    encode_piece(coded_ref, weighted, row)


def weigh(pieces, weight, *products):
    rows, obs = pieces[REACH].shape
    return pl.pallas_call(
        weigh_kernel,
        out_shape=(
            jax.ShapeDtypeStruct((rows + EXTRA, obs), BF16),
            jax.ShapeDtypeStruct((rows, obs), F32),
            jax.ShapeDtypeStruct((8, obs), F32),
        ),
        in_specs=[vmem()] * (OFFSETS + 1 + len(products)),
        out_specs=(vmem(),) * 3,
        compiler_params=kernel_params(),
        name="weigh",
    )(*pieces, weight, *products)


def finish_kernel(edge, starts, field_ref, first_ref, last_ref, steps_ref, *refs):
    tails, refs = refs[: len(starts)], refs[len(starts) :]
    start_ref, image_ref, start_low_ref, image_low_ref, increment_ref, residual_ref, dots = refs
    lat, members, lon = field_ref.shape
    row = jnp.zeros((8, dots.shape[0]), F32)
    for tail, (begin, parted) in zip(tails, starts):
        row = row + (carried_row(tail, begin, 8) if parted else tail[pl.ds(begin, 8), :])
    square = (dots.shape[0], dots.shape[0])
    diagonal = lax.broadcasted_iota(jnp.int32, square, 0) == lax.broadcasted_iota(jnp.int32, square, 1)
    dots[...] = jnp.sum(jnp.where(diagonal, row[0:1], 0.0), axis=1, keepdims=True)

    @pl.loop(0, members // 8)
    def _(index):
        begin = pl.multiple_of(index * 8, 8)
        group = pl.ds(begin, 8)
        coefs = coefficients(steps_ref, group)
        rows = extended_rows(field_ref, first_ref, last_ref, edge, group)
        rows = spread_steps(rows, coefs)
        pp, pg, gg, gh = [dots[pl.ds(begin + k * members, 8), :] for k in range(4)]
        step0 = pp / (pp + pg)
        u, w = 1.0 - step0, -step0
        norm1 = u * u * pp + 2.0 * u * w * pg + w * w * gg
        x = u + norm1 / pp
        curve = x * (x * pp + (x + w) * pg + w * gg) + w * (x * pg + (x + w) * gg + w * gh)
        step1 = norm1 / curve
        inc_p, inc_g = step0 + step1 * x, step1 * w
        res_p, res_g, res_h = u - step1 * x, w - step1 * (x + w), -step1 * w
        for row in range(lat):
            increment_ref[group, row, :] = (
                inc_p * start_low_ref[row, group, :] + inc_g * image_low_ref[row, group, :]
            )
            residual_ref[group, row, :] = (
                res_p * start_ref[row, group, :]
                + res_g * image_ref[row, group, :]
                + res_h * rows[row][:, :lon]
            )


def finish(field, first, last, steps, tails, start, image, start_low, image_low, edge):
    lat, members, lon = field.shape
    out = jax.ShapeDtypeStruct((members, lat, lon), F32)
    starts = [place for _, *place in tails]
    return pl.pallas_call(
        functools.partial(finish_kernel, edge, starts),
        out_shape=(out, out),
        in_specs=[vmem()] * (8 + len(tails)),
        out_specs=(vmem(), vmem()),
        scratch_shapes=[pltpu.VMEM((4 * members, 1), F32)],
        compiler_params=kernel_params(),
        name="finish",
    )(field, first, last, steps, *[part for part, *_ in tails], start, image, start_low, image_low)


def local(footprints, slot_target, slot_count, step_count, sigma, innovations, obs_weight):
    tiles = footprints[0, 0]
    slots, obs, lat, lon = tiles.shape
    blocks = innovations.shape[0]
    members = step_count.shape[0]
    count = 2 * blocks
    rows = count * members
    mine = lax.axis_index("obs").astype(jnp.int32).reshape(1)
    packet, kept, steps = prepare(mine, slot_target, slot_count, step_count, innovations, obs_weight)
    got = shifted(packet, "obs", 1)
    base = blocks * members
    weight = jnp.concatenate([packet[base : base + blocks], got[base : base + blocks]])
    facts = jnp.stack([packet[base + blocks], got[base + blocks]])
    targets = facts[:, :slots].astype(jnp.int32)
    live = facts[:, slots : 2 * slots]
    start_blocks = jnp.concatenate([kept, got[:base]]).astype(BF16)
    other = flatten_tiles(shifted(tiles, "obs", 1))
    own = flatten_tiles(in_hbm(tiles))

    def nearby(block, plain):
        return [plain if k == REACH else shifted(block, "flux", REACH - k) for k in range(OFFSETS)]

    def back(pieces, edge, carry=False):
        field, first, last = adjoint(
            pieces, targets, live, own, other, sigma, count, members, edge, carry
        )
        return field, shifted(first, "flux", -1), shifted(last, "flux", 1)

    def home(pieces):
        return [
            piece if k == REACH else shifted(piece, "flux", k - REACH) for k, piece in enumerate(pieces)
        ]

    def ahead(field, first, last, *before):
        return forward(
            field, first, last, steps, sigma, own, other, targets, live, count, wide, *before
        )

    wide = 2 * KMAX
    start, start_low, first_dots, *pieces = ahead(*back(nearby(start_blocks, start_blocks), wide))
    coded, plain, _ = weigh(home(pieces), weight)
    image, image_low, dots, *pieces = ahead(*back(nearby(coded, plain), wide), start)
    coded, plain, row = weigh(home(pieces), weight, first_dots, dots)
    pieces = nearby(coded, plain)
    if lax.axis_size("flux") == 8:
        tails = [(piece, rows, True) for k, piece in enumerate(pieces) if k != REACH]
        tails = tails + [(row, 0, False), (shifted(row, "flux", 4), 0, False)]
        field, first, last = back(pieces, KMAX, True)
        tails = tails + [(first, members, False), (last, members, False)]
    else:
        tails = [(lax.psum(row, "flux"), 0, False)]
        field, first, last = back(pieces, KMAX)
    return finish(field, first, last, steps, tails, start, image, start_low, image_low, KMAX)


def solution(mesh):
    return jax.shard_map(
        local,
        mesh=mesh,
        in_specs=(
            P(("group", "flux"), "obs", None, None, None, None),
            P(("group", "flux"), "obs", None),
            P(("group", "flux"), "obs"),
            P(("group", "obs")),
            P("group", "flux"),
            P(("group", "flux", "obs"), None, None),
            P(("group", "flux", "obs"), None),
        ),
        out_specs=(P(("group", "obs"), None, "flux"), P(("group", "obs"), None, "flux")),
        check_vma=False,
    )
```

```python
import functools

import jax
import jax.numpy as jnp
from jax import lax
from jax.experimental import pallas as pl
from jax.experimental.pallas import tpu as pltpu
from jax.sharding import PartitionSpec as P

REACH = 2
KMAX = 4
OFFSETS = 2 * REACH + 1
SPREAD = 0.24
F32 = jnp.float32
BF16 = jnp.bfloat16
VMEM_LIMIT = 16 * 1024 * 1024
STRIDE = 3
EXTRA = 16
TOP = 250.0
MIDDLE = 125.0


def shifted(block, axis, distance):
    size = lax.axis_size(axis)
    return lax.ppermute(block, axis, [(i, (i + distance) % size) for i in range(size)])


def kernel_params(**more):
    return pltpu.CompilerParams(vmem_limit_bytes=VMEM_LIMIT, **more)


def vmem():
    return pl.BlockSpec(memory_space=pltpu.VMEM)


def smem():
    return pl.BlockSpec(memory_space=pltpu.SMEM)


def flatten_kernel(pitch, tile_ref, out_ref, held, wide, sems):
    slots, obs, lat, lon = tile_ref.shape
    copies = [
        pltpu.make_async_copy(tile_ref.at[slot], held.at[slot], sems.at[slot]) for slot in range(slots)
    ]
    for copy in copies:
        copy.start()
    for slot, copy in enumerate(copies):
        copy.wait()
        for start in range(0, obs, 16):
            side = start // 16 % 2
            for k in range(16):
                wide[side, pl.ds(k * pitch, lat, stride=STRIDE), :] = held[slot, start + k].astype(F32)
            for row in range(lat):
                part = wide[side, pl.ds(row * STRIDE, 16, stride=pitch), :]
                out_ref[pl.ds(slot * obs + start, 16), pl.ds(row * lon, lon)] = part.astype(BF16)


def flatten_tiles(tiles):
    slots, obs, lat, lon = tiles.shape
    pitch = (lat * STRIDE) | 1
    return pl.pallas_call(
        functools.partial(flatten_kernel, pitch),
        out_shape=jax.ShapeDtypeStruct((slots * obs, lat * lon), BF16),
        in_specs=[pl.BlockSpec(memory_space=pltpu.HBM)],
        out_specs=vmem(),
        scratch_shapes=[
            pltpu.VMEM(tiles.shape, BF16),
            pltpu.VMEM((2, 16 * pitch, lon), F32),
            pltpu.SemaphoreType.DMA((slots,)),
        ],
        compiler_params=kernel_params(),
        cost_estimate=pl.CostEstimate(flops=0, bytes_accessed=4 * tiles.size, transcendentals=0),
        name="flatten_tiles",
    )(tiles)


def prepare_kernel(mine_ref, count_ref, *refs):
    sources, outs, held, sems = refs[:4], refs[4:7], refs[7:11], refs[11]
    packet_ref, kept_ref, table_ref = outs
    target_ref, steps_ref, innovation_ref, weight_ref = held
    blocks, _, obs = innovation_ref.shape
    members = table_ref.shape[0]
    slots = target_ref.shape[2]
    copies = [pltpu.make_async_copy(a, b, sems.at[k]) for k, (a, b) in enumerate(zip(sources, held))]
    for copy in copies:
        copy.start()
    for copy in copies:
        copy.wait()
    for member in range(members):
        table_ref[pl.ds(member, 1), :] = jnp.full((1, obs), steps_ref[member].astype(F32))
    lane = lax.broadcasted_iota(jnp.int32, (1, obs), 1)
    facts = jnp.zeros((1, obs), F32)
    for slot in range(slots):
        facts = jnp.where(lane == slot, target_ref[0, 0, slot].astype(F32), facts)
        alive = jnp.where(slot < count_ref[0, 0], 1.0, 0.0)
        facts = jnp.where(lane == slots + slot, alive, facts)
    mine = mine_ref[0]
    for block in range(blocks):
        rows = pl.ds(block * members, members)
        halves = [
            (weight_ref[pl.ds(block, 1), :] * innovation_ref[block, pl.ds(k * members, members), :])
            .astype(BF16)
            .astype(F32)
            for k in range(2)
        ]
        kept_ref[rows, :] = jnp.where(mine == 0, halves[0], halves[1])
        packet_ref[rows, :] = jnp.where(mine == 0, halves[1], halves[0])
    base = blocks * members
    packet_ref[pl.ds(base, 8), :] = jnp.concatenate(
        [weight_ref[...], facts, jnp.zeros((8 - blocks - 1, obs), F32)], axis=0
    )


def in_hbm(value):
    return pltpu.with_memory_space_constraint(value, pltpu.HBM)


def prepare(mine, targets, count, steps, innovations, weight):
    blocks, _, obs = innovations.shape
    members = steps.shape[0]
    sources = (targets, steps, innovations, weight)
    spaces = (pltpu.SMEM, pltpu.SMEM, pltpu.VMEM, pltpu.VMEM)
    return pl.pallas_call(
        prepare_kernel,
        out_shape=(
            jax.ShapeDtypeStruct((blocks * members + 8, obs), F32),
            jax.ShapeDtypeStruct((blocks * members, obs), F32),
            jax.ShapeDtypeStruct((members, obs), F32),
        ),
        in_specs=[smem()] * 2 + [pl.BlockSpec(memory_space=pltpu.HBM)] * len(sources),
        out_specs=(vmem(),) * 3,
        scratch_shapes=[space(part.shape, part.dtype) for space, part in zip(spaces, sources)]
        + [pltpu.SemaphoreType.DMA((len(sources),))],
        compiler_params=kernel_params(),
        name="prepare",
    )(mine, count, *[in_hbm(part) for part in sources])


def split(value):
    high = value.astype(BF16)
    return high, (value - high.astype(F32)).astype(BF16)


def thirds(row):
    parts = []
    for _ in range(3):
        part = row.astype(BF16).astype(F32)
        parts.append(part)
        row = row - part
    return parts


def encode(value, scale):
    level = jnp.abs(value) * (TOP / scale)
    whole = jnp.floor(level)
    code = (1.0 + level - whole) * jnp.exp2(whole - MIDDLE)
    return jnp.where(value < 0.0, -code, code).astype(BF16)


def decode(code, unit):
    code = code.astype(F32)
    size = jnp.abs(code)
    whole = jnp.floor(jnp.log2(size))
    value = (whole + (MIDDLE - 1.0) + size * jnp.exp2(-whole)) * unit
    return jnp.where(code < 0.0, -value, value)


def largest(values):
    top = jnp.max(jnp.abs(values), axis=0, keepdims=True)
    return jnp.maximum(jnp.max(top, axis=1, keepdims=True), 1e-30)


def encode_piece(out_ref, values, carried=None):
    rows, lanes = values.shape
    scale = largest(values)
    out_ref[pl.ds(0, rows), :] = encode(values, scale)
    zero = jnp.zeros((1, lanes), F32)
    lines = thirds(jnp.broadcast_to(scale, (1, lanes))) + [zero] * 5
    lines = lines + (thirds(carried) + [zero] * 5 if carried is not None else [zero] * 8)
    out_ref[pl.ds(rows, EXTRA), :] = jnp.concatenate(lines, axis=0).astype(BF16)


def carried_row(ref, rows, begin):
    lines = ref[pl.ds(rows, EXTRA), :].astype(F32)
    return lines[begin : begin + 1] + lines[begin + 1 : begin + 2] + lines[begin + 2 : begin + 3]


def decode_piece(ref, rows):
    unit = carried_row(ref, rows, 0) * (1.0 / TOP)
    return decode(ref[pl.ds(0, rows), :], unit)


def adjoint_kernel(edge, coded, flux_ref, target_ref, live_ref, blocks_ref, *refs):
    own_ref, other_ref, sigma_ref, field_ref, first_ref, last_ref, near, picked = refs
    bands = blocks_ref.shape[0]
    members = picked.shape[0] // 2
    obs = blocks_ref.shape[2]
    rows = near.shape[0] // OFFSETS
    count = rows // members
    slots = own_ref.shape[0] // obs
    lat, lon = sigma_ref.shape
    for offset in range(OFFSETS):
        band = lax.rem(flux_ref[0] + (bands + offset - REACH), bands)
        if coded:
            block = decode_piece(blocks_ref.at[band], rows)
        else:
            block = blocks_ref[band].astype(F32)
        near[pl.ds(offset * rows, rows), :] = block
    for side in range(2):
        for slot in range(slots):
            target = target_ref[side, slot]
            place = (target // 2) * count + side * 2 + target % 2
            block = near[pl.ds(pl.multiple_of(place * members, members), members), :] * live_ref[side, slot]
            high, low = split(block)
            columns = pl.ds((side * slots + slot) * obs, obs)
            picked[pl.ds(0, members), columns] = high
            picked[pl.ds(members, members), columns] = low
    half = slots * obs
    for row in range(0, lat, 2):
        cells = pl.ds(row * lon, 2 * lon)
        both = jnp.dot(picked[:, :half], own_ref[:, cells], preferred_element_type=F32)
        both = both + jnp.dot(picked[:, half:], other_ref[:, cells], preferred_element_type=F32)
        total = both[:members] + both[members:]
        for k in range(2):
            field = total[:, k * lon : (k + 1) * lon] * sigma_ref[row + k, :][None, :]
            field_ref[row + k] = field
            span = pl.ds((row + k) * edge, edge)
            first_ref[:, span] = field[:, :edge]
            last_ref[:, span] = field[:, lon - edge :]


def adjoint(band, blocks, targets, live, own, other, sigma, count, members, edge):
    obs = blocks.shape[2]
    lat, lon = sigma.shape
    coded = blocks.shape[1] > count * members
    edges = jax.ShapeDtypeStruct((members, lat * edge), F32)
    return pl.pallas_call(
        functools.partial(adjoint_kernel, edge, coded),
        out_shape=(jax.ShapeDtypeStruct((lat, members, lon), F32), edges, edges),
        in_specs=[smem()] * 3 + [vmem()] * 4,
        out_specs=(vmem(), vmem(), vmem()),
        scratch_shapes=[
            pltpu.VMEM((OFFSETS * count * members, obs), F32),
            pltpu.VMEM((2 * members, 2 * own.shape[0]), BF16),
        ],
        compiler_params=kernel_params(),
        cost_estimate=pl.CostEstimate(
            flops=8 * members * own.size, bytes_accessed=4 * own.size, transcendentals=0
        ),
        name="adjoint",
    )(band, targets, live, blocks, own, other, sigma)


def spread_steps(rows, coefs):
    zero = jnp.zeros_like(rows[0])
    lanes = rows[0].shape[1]
    for coef in coefs:
        keep = 1.0 - 4.0 * coef
        padded = [zero] + rows + [zero]
        rows = [
            keep * padded[i]
            + coef
            * (
                (padded[i - 1] + padded[i + 1])
                + (pltpu.roll(padded[i], 1, 1) + pltpu.roll(padded[i], lanes - 1, 1))
            )
            for i in range(1, len(rows) + 1)
        ]
    return rows


def extended_rows(field_ref, first_ref, last_ref, edge, group):
    lat, _, lon = field_ref.shape
    rows = []
    for row in range(lat):
        after = first_ref[group, pl.ds(row * edge, edge)]
        before = last_ref[group, pl.ds(row * edge, edge)]
        gap = jnp.zeros((8, lon - 2 * edge), F32)
        rows.append(jnp.concatenate([field_ref[row, group, :], after, gap, before], axis=1))
    return rows


def coefficients(steps_ref, group):
    steps = steps_ref[group, pl.ds(0, 1)]
    return [jnp.where(steps > step + 0.5, SPREAD, 0.0).astype(F32) for step in range(KMAX)]


def forward_kernel(edge, second, target_ref, live_ref, *refs):
    field_ref, first_ref, last_ref, steps_ref, sigma_ref, own_ref, other_ref = refs[:7]
    refs = refs[7:]
    if second:
        before_ref, refs = refs[0], refs[1:]
    upper_ref, lower_ref, dots_ref = refs[:3]
    pieces = refs[3 : 3 + OFFSETS]
    halves, sums = refs[3 + OFFSETS :]
    lat, members, lon = field_ref.shape
    obs = sums.shape[1]
    slots = own_ref.shape[0] // obs
    rows = sums.shape[0] // OFFSETS
    count = rows // members

    @pl.loop(0, members // 8)
    def _(index):
        group = pl.ds(pl.multiple_of(index * 8, 8), 8)
        coefs = coefficients(steps_ref, group)
        rows = extended_rows(field_ref, first_ref, last_ref, edge, group)
        rows = spread_steps(rows, coefs)
        square = jnp.zeros((8, lon), F32)
        cross = jnp.zeros((8, lon), F32)
        for row in range(lat):
            own_cells = rows[row][:, :lon]
            upper_ref[row, group, :] = own_cells
            square = square + own_cells * own_cells
            if second:
                cross = cross + own_cells * before_ref[row, group, :]
        dots_ref[0, group, :] = square
        if second:
            dots_ref[1, group, :] = cross
        rows = spread_steps(rows, coefs)
        for row in range(lat):
            low_field = rows[row][:, :lon] * sigma_ref[row, :][None, :]
            lower_ref[row, group, :] = low_field

    for row in range(lat):
        high, low = split(lower_ref[row])
        halves[pl.ds(0, members), pl.ds(row * lon, lon)] = high
        halves[pl.ds(members, members), pl.ds(row * lon, lon)] = low
    sums[...] = jnp.zeros_like(sums)
    contract = (((1,), (1,)), ((), ()))
    for side, tile_ref in enumerate((own_ref, other_ref)):
        for slot in range(0, slots, 2):
            both = lax.dot_general(
                halves[...], tile_ref[pl.ds(slot * obs, 2 * obs), :], contract, preferred_element_type=F32
            )
            total = both[:members] + both[members:]
            for k in range(2):
                target = target_ref[side, slot + k]
                place = (target // 2) * count + side * 2 + target % 2
                block = pl.ds(pl.multiple_of(place * members, members), members)
                sums[block, :] = (
                    sums[block, :] + total[:, k * obs : (k + 1) * obs] * live_ref[side, slot + k]
                )
    for offset in range(OFFSETS):
        values = sums[pl.ds(offset * rows, rows), :]
        if offset == REACH:
            pieces[offset][...] = values
        else:
            encode_piece(pieces[offset], values)


def forward(field, first, last, steps, sigma, own, other, targets, live, count, edge, before=None):
    lat, members, lon = field.shape
    obs = own.shape[0] // targets.shape[1]
    more = () if before is None else (before,)
    shape = jax.ShapeDtypeStruct((lat, members, lon), F32)
    pieces = [jax.ShapeDtypeStruct((count * members + EXTRA, obs), BF16) for _ in range(OFFSETS)]
    pieces[REACH] = jax.ShapeDtypeStruct((count * members, obs), F32)
    dots = jax.ShapeDtypeStruct((1 + len(more), members, lon), F32)
    return pl.pallas_call(
        functools.partial(forward_kernel, edge, before is not None),
        out_shape=(shape, shape, dots, *pieces),
        in_specs=[smem(), smem()] + [vmem()] * (7 + len(more)),
        out_specs=(vmem(),) * (3 + OFFSETS),
        scratch_shapes=[
            pltpu.VMEM((2 * members, lat * lon), BF16),
            pltpu.VMEM((OFFSETS * count * members, obs), F32),
        ],
        compiler_params=kernel_params(),
        cost_estimate=pl.CostEstimate(
            flops=8 * members * own.size, bytes_accessed=4 * own.size, transcendentals=0
        ),
        name="forward",
    )(targets, live, field, first, last, steps, sigma, own, other, *more)


def weigh_kernel(*refs):
    pieces = refs[:OFFSETS]
    weight_ref, refs = refs[OFFSETS], refs[OFFSETS + 1 :]
    products, coded_ref = refs[:-1], refs[-1]
    count = weight_ref.shape[0]
    rows, obs = pieces[REACH].shape
    members = rows // count
    total = pieces[REACH][...]
    for offset in range(OFFSETS):
        if offset != REACH:
            total = total + decode_piece(pieces[offset], rows)
    weight = jnp.concatenate(
        [jnp.broadcast_to(weight_ref[pl.ds(block, 1), :], (members, obs)) for block in range(count)], axis=0
    )
    weighted = total * weight
    row = None
    if products:
        first_ref, second_ref = products
        curve = (total * weighted).reshape(count, members, obs)
        parts = jnp.concatenate(
            [first_ref[0], second_ref[1], second_ref[0], jnp.sum(curve, axis=0)], axis=0
        )
        row = lax.dot_general(
            jnp.ones((8, obs), F32),
            parts,
            (((1,), (1,)), ((), ())),
            precision=lax.Precision.HIGHEST,
            preferred_element_type=F32,
        )[:1]
    encode_piece(coded_ref, weighted, row)


def weigh(pieces, weight, *products):
    rows, obs = pieces[REACH].shape
    return pl.pallas_call(
        weigh_kernel,
        out_shape=jax.ShapeDtypeStruct((rows + EXTRA, obs), BF16),
        in_specs=[vmem()] * (OFFSETS + 1 + len(products)),
        out_specs=vmem(),
        compiler_params=kernel_params(),
        name="weigh",
    )(*pieces, weight, *products)


def finish_kernel(edge, field_ref, first_ref, last_ref, steps_ref, blocks_ref, *refs):
    start_ref, image_ref, start_low_ref, image_low_ref, increment_ref, residual_ref, dots = refs
    lat, members, lon = field_ref.shape
    row = jnp.zeros((1, dots.shape[0]), F32)
    for band in range(blocks_ref.shape[0]):
        row = row + carried_row(blocks_ref.at[band], blocks_ref.shape[1] - EXTRA, 8)
    square = (dots.shape[0], dots.shape[0])
    diagonal = lax.broadcasted_iota(jnp.int32, square, 0) == lax.broadcasted_iota(jnp.int32, square, 1)
    dots[...] = jnp.sum(jnp.where(diagonal, row, 0.0), axis=1, keepdims=True)

    @pl.loop(0, members // 8)
    def _(index):
        begin = pl.multiple_of(index * 8, 8)
        group = pl.ds(begin, 8)
        coefs = coefficients(steps_ref, group)
        rows = extended_rows(field_ref, first_ref, last_ref, edge, group)
        rows = spread_steps(rows, coefs)
        pp, pg, gg, gh = [dots[pl.ds(begin + k * members, 8), :] for k in range(4)]
        step0 = pp / (pp + pg)
        u, w = 1.0 - step0, -step0
        norm1 = u * u * pp + 2.0 * u * w * pg + w * w * gg
        x = u + norm1 / pp
        curve = x * (x * pp + (x + w) * pg + w * gg) + w * (x * pg + (x + w) * gg + w * gh)
        step1 = norm1 / curve
        inc_p, inc_g = step0 + step1 * x, step1 * w
        res_p, res_g, res_h = u - step1 * x, w - step1 * (x + w), -step1 * w
        for row in range(lat):
            increment_ref[group, row, :] = (
                inc_p * start_low_ref[row, group, :] + inc_g * image_low_ref[row, group, :]
            )
            residual_ref[group, row, :] = (
                res_p * start_ref[row, group, :]
                + res_g * image_ref[row, group, :]
                + res_h * rows[row][:, :lon]
            )


def finish(field, first, last, steps, blocks, start, image, start_low, image_low, edge):
    lat, members, lon = field.shape
    out = jax.ShapeDtypeStruct((members, lat, lon), F32)
    return pl.pallas_call(
        functools.partial(finish_kernel, edge),
        out_shape=(out, out),
        in_specs=[vmem()] * 9,
        out_specs=(vmem(), vmem()),
        scratch_shapes=[pltpu.VMEM((4 * members, 1), F32)],
        compiler_params=kernel_params(),
        name="finish",
    )(field, first, last, steps, blocks, start, image, start_low, image_low)


def local(footprints, slot_target, slot_count, step_count, sigma, innovations, obs_weight):
    tiles = footprints[0, 0]
    slots, obs, lat, lon = tiles.shape
    blocks = innovations.shape[0]
    members = step_count.shape[0]
    count = 2 * blocks
    band = lax.axis_index("flux").astype(jnp.int32).reshape(1)
    mine = lax.axis_index("obs").astype(jnp.int32).reshape(1)
    packet, kept, steps = prepare(mine, slot_target, slot_count, step_count, innovations, obs_weight)
    got = shifted(packet, "obs", 1)
    base = blocks * members
    weight = jnp.concatenate([packet[base : base + blocks], got[base : base + blocks]])
    facts = jnp.stack([packet[base + blocks], got[base + blocks]])
    targets = facts[:, :slots].astype(jnp.int32)
    live = facts[:, slots : 2 * slots]
    start_blocks = jnp.concatenate([kept, got[:base]]).astype(BF16)
    other = flatten_tiles(shifted(tiles, "obs", 1))
    own = flatten_tiles(in_hbm(tiles))

    def back(blocks, edge):
        blocks = lax.all_gather(blocks, "flux")
        field, first, last = adjoint(
            band, blocks, targets, live, own, other, sigma, count, members, edge
        )
        return blocks, field, shifted(first, "flux", -1), shifted(last, "flux", 1)

    def home(pieces):
        return [
            piece if k == REACH else shifted(piece, "flux", k - REACH) for k, piece in enumerate(pieces)
        ]

    def ahead(field, first, last, *before):
        return forward(
            field, first, last, steps, sigma, own, other, targets, live, count, wide, *before
        )

    wide = 2 * KMAX
    start, start_low, first_dots, *pieces = ahead(*back(start_blocks, wide)[1:])
    image, image_low, dots, *pieces = ahead(*back(weigh(home(pieces), weight), wide)[1:], start)
    blocks, field, first, last = back(weigh(home(pieces), weight, first_dots, dots), KMAX)
    return finish(field, first, last, steps, blocks, start, image, start_low, image_low, KMAX)


def solution(mesh):
    return jax.shard_map(
        local,
        mesh=mesh,
        in_specs=(
            P(("group", "flux"), "obs", None, None, None, None),
            P(("group", "flux"), "obs", None),
            P(("group", "flux"), "obs"),
            P(("group", "obs")),
            P("group", "flux"),
            P(("group", "flux", "obs"), None, None),
            P(("group", "flux", "obs"), None),
        ),
        out_specs=(P(("group", "obs"), None, "flux"), P(("group", "obs"), None, "flux")),
        check_vma=False,
    )
```

```python
import functools

import jax
import jax.numpy as jnp
from jax import lax
from jax.experimental import pallas as pl
from jax.experimental.pallas import tpu as pltpu
from jax.sharding import PartitionSpec as P

REACH = 2
KMAX = 4
OFFSETS = 2 * REACH + 1
SPREAD = 0.24
F32 = jnp.float32
BF16 = jnp.bfloat16
VMEM_LIMIT = 16 * 1024 * 1024
STRIDE = 3
EXTRA = 16
TOP = 250.0
MIDDLE = 125.0


def shifted(block, axis, distance):
    size = lax.axis_size(axis)
    return lax.ppermute(block, axis, [(i, (i + distance) % size) for i in range(size)])


def kernel_params(**more):
    return pltpu.CompilerParams(vmem_limit_bytes=VMEM_LIMIT, **more)


def vmem():
    return pl.BlockSpec(memory_space=pltpu.VMEM)


def smem():
    return pl.BlockSpec(memory_space=pltpu.SMEM)


def flatten_kernel(pitch, tile_ref, out_ref, held, wide, sems):
    slots, obs, lat, lon = tile_ref.shape
    copies = [
        pltpu.make_async_copy(tile_ref.at[slot], held.at[slot], sems.at[slot]) for slot in range(slots)
    ]
    for copy in copies:
        copy.start()
    for slot, copy in enumerate(copies):
        copy.wait()
        for start in range(0, obs, 16):
            side = start // 16 % 2
            for k in range(16):
                wide[side, pl.ds(k * pitch, lat, stride=STRIDE), :] = held[slot, start + k].astype(F32)
            for row in range(lat):
                part = wide[side, pl.ds(row * STRIDE, 16, stride=pitch), :]
                out_ref[pl.ds(slot * obs + start, 16), pl.ds(row * lon, lon)] = part.astype(BF16)


def flatten_tiles(tiles):
    slots, obs, lat, lon = tiles.shape
    pitch = (lat * STRIDE) | 1
    return pl.pallas_call(
        functools.partial(flatten_kernel, pitch),
        out_shape=jax.ShapeDtypeStruct((slots * obs, lat * lon), BF16),
        in_specs=[pl.BlockSpec(memory_space=pltpu.HBM)],
        out_specs=vmem(),
        scratch_shapes=[
            pltpu.VMEM(tiles.shape, BF16),
            pltpu.VMEM((2, 16 * pitch, lon), F32),
            pltpu.SemaphoreType.DMA((slots,)),
        ],
        compiler_params=kernel_params(),
        cost_estimate=pl.CostEstimate(flops=0, bytes_accessed=4 * tiles.size, transcendentals=0),
        name="flatten_tiles",
    )(tiles)


def prepare_kernel(mine_ref, count_ref, *refs):
    sources, outs, held, sems = refs[:4], refs[4:7], refs[7:11], refs[11]
    packet_ref, kept_ref, table_ref = outs
    target_ref, steps_ref, innovation_ref, weight_ref = held
    blocks, _, obs = innovation_ref.shape
    members = table_ref.shape[0]
    slots = target_ref.shape[2]
    copies = [pltpu.make_async_copy(a, b, sems.at[k]) for k, (a, b) in enumerate(zip(sources, held))]
    for copy in copies:
        copy.start()
    for copy in copies:
        copy.wait()
    for member in range(members):
        table_ref[pl.ds(member, 1), :] = jnp.full((1, obs), steps_ref[member].astype(F32))
    lane = lax.broadcasted_iota(jnp.int32, (1, obs), 1)
    facts = jnp.zeros((1, obs), F32)
    for slot in range(slots):
        facts = jnp.where(lane == slot, target_ref[0, 0, slot].astype(F32), facts)
        alive = jnp.where(slot < count_ref[0, 0], 1.0, 0.0)
        facts = jnp.where(lane == slots + slot, alive, facts)
    mine = mine_ref[0]
    for block in range(blocks):
        rows = pl.ds(block * members, members)
        halves = [
            (weight_ref[pl.ds(block, 1), :] * innovation_ref[block, pl.ds(k * members, members), :])
            .astype(BF16)
            .astype(F32)
            for k in range(2)
        ]
        kept_ref[rows, :] = jnp.where(mine == 0, halves[0], halves[1])
        packet_ref[rows, :] = jnp.where(mine == 0, halves[1], halves[0])
    base = blocks * members
    packet_ref[pl.ds(base, 8), :] = jnp.concatenate(
        [weight_ref[...], facts, jnp.zeros((8 - blocks - 1, obs), F32)], axis=0
    )


def in_hbm(value):
    return pltpu.with_memory_space_constraint(value, pltpu.HBM)


def prepare(mine, targets, count, steps, innovations, weight):
    blocks, _, obs = innovations.shape
    members = steps.shape[0]
    sources = (targets, steps, innovations, weight)
    spaces = (pltpu.SMEM, pltpu.SMEM, pltpu.VMEM, pltpu.VMEM)
    return pl.pallas_call(
        prepare_kernel,
        out_shape=(
            jax.ShapeDtypeStruct((blocks * members + 8, obs), F32),
            jax.ShapeDtypeStruct((blocks * members, obs), F32),
            jax.ShapeDtypeStruct((members, obs), F32),
        ),
        in_specs=[smem()] * 2 + [pl.BlockSpec(memory_space=pltpu.HBM)] * len(sources),
        out_specs=(vmem(),) * 3,
        scratch_shapes=[space(part.shape, part.dtype) for space, part in zip(spaces, sources)]
        + [pltpu.SemaphoreType.DMA((len(sources),))],
        compiler_params=kernel_params(),
        name="prepare",
    )(mine, count, *[in_hbm(part) for part in sources])


def split(value):
    high = value.astype(BF16)
    return high, (value - high.astype(F32)).astype(BF16)


def thirds(row):
    parts = []
    for _ in range(3):
        part = row.astype(BF16).astype(F32)
        parts.append(part)
        row = row - part
    return parts


def encode(value, scale):
    level = jnp.abs(value) * (TOP / scale)
    whole = jnp.floor(level)
    code = (1.0 + level - whole) * jnp.exp2(whole - MIDDLE)
    return jnp.where(value < 0.0, -code, code).astype(BF16)


def decode(code, unit):
    code = code.astype(F32)
    size = jnp.abs(code)
    whole = jnp.floor(jnp.log2(size))
    value = (whole + (MIDDLE - 1.0) + size * jnp.exp2(-whole)) * unit
    return jnp.where(code < 0.0, -value, value)


def largest(values):
    top = jnp.max(jnp.abs(values), axis=0, keepdims=True)
    return jnp.maximum(jnp.max(top, axis=1, keepdims=True), 1e-30)


def encode_piece(out_ref, values, carried=None):
    rows, lanes = values.shape
    scale = largest(values)
    out_ref[pl.ds(0, rows), :] = encode(values, scale)
    zero = jnp.zeros((1, lanes), F32)
    lines = thirds(jnp.broadcast_to(scale, (1, lanes))) + [zero] * 5
    lines = lines + (thirds(carried) + [zero] * 5 if carried is not None else [zero] * 8)
    out_ref[pl.ds(rows, EXTRA), :] = jnp.concatenate(lines, axis=0).astype(BF16)


def carried_row(ref, rows, begin):
    lines = ref[pl.ds(rows, EXTRA), :].astype(F32)
    return lines[begin : begin + 1] + lines[begin + 1 : begin + 2] + lines[begin + 2 : begin + 3]


def decode_piece(ref, rows):
    unit = carried_row(ref, rows, 0) * (1.0 / TOP)
    return decode(ref[pl.ds(0, rows), :], unit)


def adjoint_kernel(edge, coded, flux_ref, target_ref, live_ref, blocks_ref, *refs):
    own_ref, other_ref, sigma_ref, field_ref, first_ref, last_ref, near, picked = refs
    bands = blocks_ref.shape[0]
    members = picked.shape[0] // 2
    obs = blocks_ref.shape[2]
    rows = near.shape[0] // OFFSETS
    count = rows // members
    slots = own_ref.shape[0] // obs
    lat, lon = sigma_ref.shape
    for offset in range(OFFSETS):
        band = lax.rem(flux_ref[0] + (bands + offset - REACH), bands)
        if coded:
            block = decode_piece(blocks_ref.at[band], rows)
        else:
            block = blocks_ref[band].astype(F32)
        near[pl.ds(offset * rows, rows), :] = block
    for side in range(2):
        for slot in range(slots):
            target = target_ref[side, slot]
            place = (target // 2) * count + side * 2 + target % 2
            block = near[pl.ds(pl.multiple_of(place * members, members), members), :] * live_ref[side, slot]
            high, low = split(block)
            columns = pl.ds((side * slots + slot) * obs, obs)
            picked[pl.ds(0, members), columns] = high
            picked[pl.ds(members, members), columns] = low
    half = slots * obs
    for row in range(0, lat, 2):
        cells = pl.ds(row * lon, 2 * lon)
        both = jnp.dot(picked[:, :half], own_ref[:, cells], preferred_element_type=F32)
        both = both + jnp.dot(picked[:, half:], other_ref[:, cells], preferred_element_type=F32)
        total = both[:members] + both[members:]
        for k in range(2):
            field = total[:, k * lon : (k + 1) * lon] * sigma_ref[row + k, :][None, :]
            field_ref[row + k] = field
            span = pl.ds((row + k) * edge, edge)
            first_ref[:, span] = field[:, :edge]
            last_ref[:, span] = field[:, lon - edge :]


def adjoint(band, blocks, targets, live, own, other, sigma, count, members, edge):
    obs = blocks.shape[2]
    lat, lon = sigma.shape
    coded = blocks.shape[1] > count * members
    edges = jax.ShapeDtypeStruct((members, lat * edge), F32)
    return pl.pallas_call(
        functools.partial(adjoint_kernel, edge, coded),
        out_shape=(jax.ShapeDtypeStruct((lat, members, lon), F32), edges, edges),
        in_specs=[smem()] * 3 + [vmem()] * 4,
        out_specs=(vmem(), vmem(), vmem()),
        scratch_shapes=[
            pltpu.VMEM((OFFSETS * count * members, obs), F32),
            pltpu.VMEM((2 * members, 2 * own.shape[0]), BF16),
        ],
        compiler_params=kernel_params(),
        cost_estimate=pl.CostEstimate(
            flops=8 * members * own.size, bytes_accessed=4 * own.size, transcendentals=0
        ),
        name="adjoint",
    )(band, targets, live, blocks, own, other, sigma)


def spread_steps(rows, coefs):
    zero = jnp.zeros_like(rows[0])
    lanes = rows[0].shape[1]
    for coef in coefs:
        keep = 1.0 - 4.0 * coef
        padded = [zero] + rows + [zero]
        rows = [
            keep * padded[i]
            + coef
            * (
                (padded[i - 1] + padded[i + 1])
                + (pltpu.roll(padded[i], 1, 1) + pltpu.roll(padded[i], lanes - 1, 1))
            )
            for i in range(1, len(rows) + 1)
        ]
    return rows


def extended_rows(field_ref, first_ref, last_ref, edge, group):
    lat, _, lon = field_ref.shape
    rows = []
    for row in range(lat):
        after = first_ref[group, pl.ds(row * edge, edge)]
        before = last_ref[group, pl.ds(row * edge, edge)]
        gap = jnp.zeros((8, lon - 2 * edge), F32)
        rows.append(jnp.concatenate([field_ref[row, group, :], after, gap, before], axis=1))
    return rows


def coefficients(steps_ref, group):
    steps = steps_ref[group, pl.ds(0, 1)]
    return [jnp.where(steps > step + 0.5, SPREAD, 0.0).astype(F32) for step in range(KMAX)]


def forward_kernel(edge, second, target_ref, live_ref, *refs):
    field_ref, first_ref, last_ref, steps_ref, sigma_ref, own_ref, other_ref = refs[:7]
    refs = refs[7:]
    if second:
        before_ref, refs = refs[0], refs[1:]
    upper_ref, lower_ref, dots_ref = refs[:3]
    pieces = refs[3 : 3 + OFFSETS]
    halves, sums = refs[3 + OFFSETS :]
    lat, members, lon = field_ref.shape
    obs = sums.shape[1]
    slots = own_ref.shape[0] // obs
    rows = sums.shape[0] // OFFSETS
    count = rows // members

    @pl.loop(0, members // 8)
    def _(index):
        group = pl.ds(pl.multiple_of(index * 8, 8), 8)
        coefs = coefficients(steps_ref, group)
        rows = extended_rows(field_ref, first_ref, last_ref, edge, group)
        rows = spread_steps(rows, coefs)
        square = jnp.zeros((8, lon), F32)
        cross = jnp.zeros((8, lon), F32)
        for row in range(lat):
            own_cells = rows[row][:, :lon]
            upper_ref[row, group, :] = own_cells
            square = square + own_cells * own_cells
            if second:
                cross = cross + own_cells * before_ref[row, group, :]
        dots_ref[0, group, :] = square
        if second:
            dots_ref[1, group, :] = cross
        rows = spread_steps(rows, coefs)
        for row in range(lat):
            low_field = rows[row][:, :lon] * sigma_ref[row, :][None, :]
            lower_ref[row, group, :] = low_field

    for row in range(lat):
        high, low = split(lower_ref[row])
        halves[pl.ds(0, members), pl.ds(row * lon, lon)] = high
        halves[pl.ds(members, members), pl.ds(row * lon, lon)] = low
    sums[...] = jnp.zeros_like(sums)
    contract = (((1,), (1,)), ((), ()))
    for side, tile_ref in enumerate((own_ref, other_ref)):
        for slot in range(0, slots, 2):
            both = lax.dot_general(
                halves[...], tile_ref[pl.ds(slot * obs, 2 * obs), :], contract, preferred_element_type=F32
            )
            total = both[:members] + both[members:]
            for k in range(2):
                target = target_ref[side, slot + k]
                place = (target // 2) * count + side * 2 + target % 2
                block = pl.ds(pl.multiple_of(place * members, members), members)
                sums[block, :] = (
                    sums[block, :] + total[:, k * obs : (k + 1) * obs] * live_ref[side, slot + k]
                )
    for offset in range(OFFSETS):
        values = sums[pl.ds(offset * rows, rows), :]
        if offset == REACH:
            pieces[offset][...] = values
        else:
            encode_piece(pieces[offset], values)


def forward(field, first, last, steps, sigma, own, other, targets, live, count, edge, before=None):
    lat, members, lon = field.shape
    obs = own.shape[0] // targets.shape[1]
    more = () if before is None else (before,)
    shape = jax.ShapeDtypeStruct((lat, members, lon), F32)
    pieces = [jax.ShapeDtypeStruct((count * members + EXTRA, obs), BF16) for _ in range(OFFSETS)]
    pieces[REACH] = jax.ShapeDtypeStruct((count * members, obs), F32)
    dots = jax.ShapeDtypeStruct((1 + len(more), members, lon), F32)
    return pl.pallas_call(
        functools.partial(forward_kernel, edge, before is not None),
        out_shape=(shape, shape, dots, *pieces),
        in_specs=[smem(), smem()] + [vmem()] * (7 + len(more)),
        out_specs=(vmem(),) * (3 + OFFSETS),
        scratch_shapes=[
            pltpu.VMEM((2 * members, lat * lon), BF16),
            pltpu.VMEM((OFFSETS * count * members, obs), F32),
        ],
        compiler_params=kernel_params(),
        cost_estimate=pl.CostEstimate(
            flops=8 * members * own.size, bytes_accessed=4 * own.size, transcendentals=0
        ),
        name="forward",
    )(targets, live, field, first, last, steps, sigma, own, other, *more)


def weigh_kernel(*refs):
    pieces = refs[:OFFSETS]
    weight_ref, refs = refs[OFFSETS], refs[OFFSETS + 1 :]
    products, coded_ref = refs[:-1], refs[-1]
    count = weight_ref.shape[0]
    rows, obs = pieces[REACH].shape
    members = rows // count
    total = pieces[REACH][...]
    for offset in range(OFFSETS):
        if offset != REACH:
            total = total + decode_piece(pieces[offset], rows)
    weight = jnp.concatenate(
        [jnp.broadcast_to(weight_ref[pl.ds(block, 1), :], (members, obs)) for block in range(count)], axis=0
    )
    weighted = total * weight
    row = None
    if products:
        first_ref, second_ref = products
        curve = (total * weighted).reshape(count, members, obs)
        parts = jnp.concatenate(
            [first_ref[0], second_ref[1], second_ref[0], jnp.sum(curve, axis=0)], axis=0
        )
        row = lax.dot_general(
            jnp.ones((8, obs), F32),
            parts,
            (((1,), (1,)), ((), ())),
            precision=lax.Precision.HIGHEST,
            preferred_element_type=F32,
        )[:1]
    encode_piece(coded_ref, weighted, row)


def weigh(pieces, weight, *products):
    rows, obs = pieces[REACH].shape
    return pl.pallas_call(
        weigh_kernel,
        out_shape=jax.ShapeDtypeStruct((rows + EXTRA, obs), BF16),
        in_specs=[vmem()] * (OFFSETS + 1 + len(products)),
        out_specs=vmem(),
        compiler_params=kernel_params(),
        name="weigh",
    )(*pieces, weight, *products)


def finish_kernel(edge, field_ref, first_ref, last_ref, steps_ref, blocks_ref, *refs):
    start_ref, image_ref, start_low_ref, image_low_ref, increment_ref, residual_ref, dots = refs
    lat, members, lon = field_ref.shape
    row = jnp.zeros((1, dots.shape[0]), F32)
    for band in range(blocks_ref.shape[0]):
        row = row + carried_row(blocks_ref.at[band], blocks_ref.shape[1] - EXTRA, 8)
    square = (dots.shape[0], dots.shape[0])
    diagonal = lax.broadcasted_iota(jnp.int32, square, 0) == lax.broadcasted_iota(jnp.int32, square, 1)
    dots[...] = jnp.sum(jnp.where(diagonal, row, 0.0), axis=1, keepdims=True)

    @pl.loop(0, members // 8)
    def _(index):
        begin = pl.multiple_of(index * 8, 8)
        group = pl.ds(begin, 8)
        coefs = coefficients(steps_ref, group)
        rows = extended_rows(field_ref, first_ref, last_ref, edge, group)
        rows = spread_steps(rows, coefs)
        pp, pg, gg, gh = [dots[pl.ds(begin + k * members, 8), :] for k in range(4)]
        step0 = pp / (pp + pg)
        u, w = 1.0 - step0, -step0
        norm1 = u * u * pp + 2.0 * u * w * pg + w * w * gg
        x = u + norm1 / pp
        curve = x * (x * pp + (x + w) * pg + w * gg) + w * (x * pg + (x + w) * gg + w * gh)
        step1 = norm1 / curve
        inc_p, inc_g = step0 + step1 * x, step1 * w
        res_p, res_g, res_h = u - step1 * x, w - step1 * (x + w), -step1 * w
        for row in range(lat):
            increment_ref[group, row, :] = (
                inc_p * start_low_ref[row, group, :] + inc_g * image_low_ref[row, group, :]
            )
            residual_ref[group, row, :] = (
                res_p * start_ref[row, group, :]
                + res_g * image_ref[row, group, :]
                + res_h * rows[row][:, :lon]
            )


def finish(field, first, last, steps, blocks, start, image, start_low, image_low, edge):
    lat, members, lon = field.shape
    out = jax.ShapeDtypeStruct((members, lat, lon), F32)
    return pl.pallas_call(
        functools.partial(finish_kernel, edge),
        out_shape=(out, out),
        in_specs=[vmem()] * 9,
        out_specs=(vmem(), vmem()),
        scratch_shapes=[pltpu.VMEM((4 * members, 1), F32)],
        compiler_params=kernel_params(),
        name="finish",
    )(field, first, last, steps, blocks, start, image, start_low, image_low)


def local(footprints, slot_target, slot_count, step_count, sigma, innovations, obs_weight):
    tiles = footprints[0, 0]
    slots, obs, lat, lon = tiles.shape
    blocks = innovations.shape[0]
    members = step_count.shape[0]
    count = 2 * blocks
    band = lax.axis_index("flux").astype(jnp.int32).reshape(1)
    mine = lax.axis_index("obs").astype(jnp.int32).reshape(1)
    packet, kept, steps = prepare(mine, slot_target, slot_count, step_count, innovations, obs_weight)
    got = shifted(packet, "obs", 1)
    base = blocks * members
    weight = jnp.concatenate([packet[base : base + blocks], got[base : base + blocks]])
    facts = jnp.stack([packet[base + blocks], got[base + blocks]])
    targets = facts[:, :slots].astype(jnp.int32)
    live = facts[:, slots : 2 * slots]
    start_blocks = jnp.concatenate([kept, got[:base]]).astype(BF16)
    other = flatten_tiles(shifted(tiles, "obs", 1))
    own = flatten_tiles(in_hbm(tiles))

    def back(blocks, edge):
        copies = jnp.broadcast_to(blocks[None], (lax.axis_size("flux"),) + blocks.shape)
        blocks = lax.all_to_all(copies, "flux", 0, 0, tiled=True)
        field, first, last = adjoint(
            band, blocks, targets, live, own, other, sigma, count, members, edge
        )
        return blocks, field, shifted(first, "flux", -1), shifted(last, "flux", 1)

    def home(pieces):
        return [
            piece if k == REACH else shifted(piece, "flux", k - REACH) for k, piece in enumerate(pieces)
        ]

    def ahead(field, first, last, *before):
        return forward(
            field, first, last, steps, sigma, own, other, targets, live, count, wide, *before
        )

    wide = 2 * KMAX
    start, start_low, first_dots, *pieces = ahead(*back(start_blocks, wide)[1:])
    image, image_low, dots, *pieces = ahead(*back(weigh(home(pieces), weight), wide)[1:], start)
    blocks, field, first, last = back(weigh(home(pieces), weight, first_dots, dots), KMAX)
    return finish(field, first, last, steps, blocks, start, image, start_low, image_low, KMAX)


def solution(mesh):
    return jax.shard_map(
        local,
        mesh=mesh,
        in_specs=(
            P(("group", "flux"), "obs", None, None, None, None),
            P(("group", "flux"), "obs", None),
            P(("group", "flux"), "obs"),
            P(("group", "obs")),
            P("group", "flux"),
            P(("group", "flux", "obs"), None, None),
            P(("group", "flux", "obs"), None),
        ),
        out_specs=(P(("group", "obs"), None, "flux"), P(("group", "obs"), None, "flux")),
        check_vma=False,
    )
```

```python
import functools

import jax
import jax.numpy as jnp
from jax import lax
from jax.experimental import pallas as pl
from jax.experimental.pallas import tpu as pltpu
from jax.sharding import PartitionSpec as P

REACH = 2
KMAX = 4
OFFSETS = 2 * REACH + 1
SPREAD = 0.24
F32 = jnp.float32
BF16 = jnp.bfloat16
VMEM_LIMIT = 16 * 1024 * 1024
STRIDE = 3
EDGE = 2 * KMAX
EXTRA = 16
TOP = 250.0
MIDDLE = 125.0


def shifted(block, axis, distance):
    size = lax.axis_size(axis)
    return lax.ppermute(block, axis, [(i, (i + distance) % size) for i in range(size)])


def kernel_params(**more):
    return pltpu.CompilerParams(vmem_limit_bytes=VMEM_LIMIT, **more)


def vmem():
    return pl.BlockSpec(memory_space=pltpu.VMEM)


def smem():
    return pl.BlockSpec(memory_space=pltpu.SMEM)


def flatten_kernel(pitch, tile_ref, out_ref, edge_ref, held, wide, pick, sems):
    slots, obs, lat, lon = tile_ref.shape
    copies = [
        pltpu.make_async_copy(tile_ref.at[slot], held.at[slot], sems.at[slot]) for slot in range(slots)
    ]
    for copy in copies:
        copy.start()
    source = lax.broadcasted_iota(jnp.int32, pick.shape, 0)
    target = lax.broadcasted_iota(jnp.int32, pick.shape, 1)
    cell = source % lon
    place = jnp.where(cell < EDGE, cell, jnp.where(cell >= lon - EDGE, cell - lon + 2 * EDGE, lon))
    chosen = (source // lon * (2 * EDGE) + place == target) & (place < lon)
    pick[...] = jnp.where(chosen, 1.0, 0.0).astype(BF16)
    for slot, copy in enumerate(copies):
        copy.wait()
        for start in range(0, obs, 16):
            side = start // 16 % 2
            for k in range(16):
                wide[side, pl.ds(k * pitch, lat, stride=STRIDE), :] = held[slot, start + k].astype(F32)
            for row in range(lat):
                part = wide[side, pl.ds(row * STRIDE, 16, stride=pitch), :]
                out_ref[pl.ds(slot * obs + start, 16), pl.ds(row * lon, lon)] = part.astype(BF16)
        for chunk in range(lat * 2 * EDGE // lon):
            rows = pl.ds(slot * obs, obs)
            source = out_ref[rows, pl.ds(chunk * pick.shape[0], pick.shape[0])]
            edge_ref[rows, pl.ds(chunk * lon, lon)] = jnp.dot(
                source, pick[...], preferred_element_type=F32
            ).astype(BF16)


def flatten_tiles(tiles):
    slots, obs, lat, lon = tiles.shape
    pitch = (lat * STRIDE) | 1
    return pl.pallas_call(
        functools.partial(flatten_kernel, pitch),
        out_shape=(
            jax.ShapeDtypeStruct((slots * obs, lat * lon), BF16),
            jax.ShapeDtypeStruct((slots * obs, lat * 2 * EDGE), BF16),
        ),
        in_specs=[pl.BlockSpec(memory_space=pltpu.HBM)],
        out_specs=(vmem(), vmem()),
        scratch_shapes=[
            pltpu.VMEM(tiles.shape, BF16),
            pltpu.VMEM((2, 16 * pitch, lon), F32),
            pltpu.VMEM((lon // (2 * EDGE) * lon, lon), BF16),
            pltpu.SemaphoreType.DMA((slots,)),
        ],
        compiler_params=kernel_params(),
        cost_estimate=pl.CostEstimate(flops=0, bytes_accessed=4 * tiles.size, transcendentals=0),
        name="flatten_tiles",
    )(tiles)


def prepare_kernel(mine_ref, count_ref, *refs):
    sources, outs, held, sems = refs[:4], refs[4:7], refs[7:11], refs[11]
    packet_ref, kept_ref, table_ref = outs
    target_ref, steps_ref, innovation_ref, weight_ref = held
    blocks, _, obs = innovation_ref.shape
    members = table_ref.shape[0]
    slots = target_ref.shape[2]
    copies = [pltpu.make_async_copy(a, b, sems.at[k]) for k, (a, b) in enumerate(zip(sources, held))]
    for copy in copies:
        copy.start()
    for copy in copies:
        copy.wait()
    for member in range(members):
        table_ref[pl.ds(member, 1), :] = jnp.full((1, obs), steps_ref[member].astype(F32))
    lane = lax.broadcasted_iota(jnp.int32, (1, obs), 1)
    facts = jnp.zeros((1, obs), F32)
    for slot in range(slots):
        facts = jnp.where(lane == slot, target_ref[0, 0, slot].astype(F32), facts)
        alive = jnp.where(slot < count_ref[0, 0], 1.0, 0.0)
        facts = jnp.where(lane == slots + slot, alive, facts)
    mine = mine_ref[0]
    for block in range(blocks):
        rows = pl.ds(block * members, members)
        halves = [
            (weight_ref[pl.ds(block, 1), :] * innovation_ref[block, pl.ds(k * members, members), :])
            .astype(BF16)
            .astype(F32)
            for k in range(2)
        ]
        kept_ref[rows, :] = jnp.where(mine == 0, halves[0], halves[1])
        packet_ref[rows, :] = jnp.where(mine == 0, halves[1], halves[0])
    base = blocks * members
    packet_ref[pl.ds(base, 8), :] = jnp.concatenate(
        [weight_ref[...], facts, jnp.zeros((8 - blocks - 1, obs), F32)], axis=0
    )


def in_hbm(value):
    return pltpu.with_memory_space_constraint(value, pltpu.HBM)


def prepare(mine, targets, count, steps, innovations, weight):
    blocks, _, obs = innovations.shape
    members = steps.shape[0]
    sources = (targets, steps, innovations, weight)
    spaces = (pltpu.SMEM, pltpu.SMEM, pltpu.VMEM, pltpu.VMEM)
    return pl.pallas_call(
        prepare_kernel,
        out_shape=(
            jax.ShapeDtypeStruct((blocks * members + 8, obs), F32),
            jax.ShapeDtypeStruct((blocks * members, obs), F32),
            jax.ShapeDtypeStruct((members, obs), F32),
        ),
        in_specs=[smem()] * 2 + [pl.BlockSpec(memory_space=pltpu.HBM)] * len(sources),
        out_specs=(vmem(),) * 3,
        scratch_shapes=[space(part.shape, part.dtype) for space, part in zip(spaces, sources)]
        + [pltpu.SemaphoreType.DMA((len(sources),))],
        compiler_params=kernel_params(),
        name="prepare",
    )(mine, count, *[in_hbm(part) for part in sources])


def split(value):
    high = value.astype(BF16)
    return high, (value - high.astype(F32)).astype(BF16)


def thirds(row):
    parts = []
    for _ in range(3):
        part = row.astype(BF16).astype(F32)
        parts.append(part)
        row = row - part
    return parts


def encode(value, scale):
    level = jnp.abs(value) * (TOP / scale)
    whole = jnp.floor(level)
    code = (1.0 + level - whole) * jnp.exp2(whole - MIDDLE)
    return jnp.where(value < 0.0, -code, code).astype(BF16)


def decode(code, unit):
    code = code.astype(F32)
    size = jnp.abs(code)
    whole = jnp.floor(jnp.log2(size))
    value = (whole + (MIDDLE - 1.0) + size * jnp.exp2(-whole)) * unit
    return jnp.where(code < 0.0, -value, value)


def largest(values):
    top = jnp.max(jnp.abs(values), axis=0, keepdims=True)
    return jnp.maximum(jnp.max(top, axis=1, keepdims=True), 1e-30)


def encode_piece(out_ref, values, carried=None):
    rows, lanes = values.shape
    scale = largest(values)
    out_ref[pl.ds(0, rows), :] = encode(values, scale)
    zero = jnp.zeros((1, lanes), F32)
    lines = thirds(jnp.broadcast_to(scale, (1, lanes))) + [zero] * 5
    lines = lines + (thirds(carried) + [zero] * 5 if carried is not None else [zero] * 8)
    out_ref[pl.ds(rows, EXTRA), :] = jnp.concatenate(lines, axis=0).astype(BF16)


def carried_row(ref, rows, begin):
    lines = ref[pl.ds(rows, EXTRA), :].astype(F32)
    return lines[begin : begin + 1] + lines[begin + 1 : begin + 2] + lines[begin + 2 : begin + 3]


def decode_piece(ref, rows):
    unit = carried_row(ref, rows, 0) * (1.0 / TOP)
    return decode(ref[pl.ds(0, rows), :], unit)


def adjoint_kernel(coded, carry, target_ref, live_ref, *refs):
    pieces = refs[:OFFSETS]
    own_ref, other_ref, sigma_ref, field_ref, first_ref, last_ref, near, picked = refs[OFFSETS:]
    members = picked.shape[0] // 2
    obs = pieces[0].shape[1]
    rows = near.shape[0] // OFFSETS
    count = rows // members
    slots = own_ref.shape[0] // obs
    lat, lon = sigma_ref.shape
    for offset in range(OFFSETS):
        if coded and offset != REACH:
            block = decode_piece(pieces[offset], rows)
        else:
            block = pieces[offset][...].astype(F32)
        near[pl.ds(offset * rows, rows), :] = block
    for side in range(2):
        for slot in range(slots):
            target = target_ref[side, slot]
            place = (target // 2) * count + side * 2 + target % 2
            block = near[pl.ds(pl.multiple_of(place * members, members), members), :] * live_ref[side, slot]
            high, low = split(block)
            columns = pl.ds((side * slots + slot) * obs, obs)
            picked[pl.ds(0, members), columns] = high
            picked[pl.ds(members, members), columns] = low
    if carry:
        tail = (pl.ds(members, 8), pl.ds(0, obs))
        first_ref[tail] = jnp.broadcast_to(carried_row(pieces[-1], rows, 8), (8, obs))
        last_ref[tail] = jnp.broadcast_to(carried_row(pieces[0], rows, 8), (8, obs))
    half = slots * obs
    for row in range(0, lat, 2):
        cells = pl.ds(row * lon, 2 * lon)
        both = jnp.dot(picked[:, :half], own_ref[:, cells], preferred_element_type=F32)
        both = both + jnp.dot(picked[:, half:], other_ref[:, cells], preferred_element_type=F32)
        total = both[:members] + both[members:]
        for k in range(2):
            field = total[:, k * lon : (k + 1) * lon] * sigma_ref[row + k, :][None, :]
            field_ref[row + k] = field
            span = pl.ds((row + k) * EDGE, EDGE)
            first_ref[pl.ds(0, members), span] = field[:, :EDGE]
            last_ref[pl.ds(0, members), span] = field[:, lon - EDGE :]


def adjoint(pieces, targets, live, own, other, sigma, count, members, carry):
    obs = pieces[0].shape[1]
    lat, lon = sigma.shape
    coded = pieces[0].shape[0] > count * members
    edges = jax.ShapeDtypeStruct((members + 8 * carry, lat * EDGE), F32)
    return pl.pallas_call(
        functools.partial(adjoint_kernel, coded, carry),
        out_shape=(
            jax.ShapeDtypeStruct((lat, members, lon), F32),
            edges,
            edges,
        ),
        in_specs=[smem(), smem()] + [vmem()] * (OFFSETS + 3),
        out_specs=(vmem(), vmem(), vmem()),
        scratch_shapes=[
            pltpu.VMEM((OFFSETS * count * members, obs), F32),
            pltpu.VMEM((2 * members, 2 * own.shape[0]), BF16),
        ],
        compiler_params=kernel_params(),
        cost_estimate=pl.CostEstimate(
            flops=8 * members * own.size, bytes_accessed=4 * own.size, transcendentals=0
        ),
        name="adjoint",
    )(targets, live, *pieces, own, other, sigma)


def spread_steps(rows, coefs):
    zero = jnp.zeros_like(rows[0])
    lanes = rows[0].shape[1]
    for coef in coefs:
        keep = 1.0 - 4.0 * coef
        padded = [zero] + rows + [zero]
        rows = [
            keep * padded[i]
            + coef
            * (
                (padded[i - 1] + padded[i + 1])
                + (pltpu.roll(padded[i], 1, 1) + pltpu.roll(padded[i], lanes - 1, 1))
            )
            for i in range(1, len(rows) + 1)
        ]
    return rows


def coefficients(steps_ref, group):
    steps = steps_ref[group, :]
    return [jnp.where(steps > step + 0.5, SPREAD, 0.0).astype(F32) for step in range(KMAX)]


def interior_kernel(second, field_ref, steps_ref, sigma_ref, own_ref, other_ref, *refs):
    if second:
        before_ref, refs = refs[0], refs[1:]
    upper_ref, lower_ref, dots_ref, part_ref, halves = refs
    lat, members, lon = field_ref.shape
    lane = lax.broadcasted_iota(jnp.int32, (8, lon), 1)
    inside = (lane >= EDGE) & (lane < lon - EDGE)

    @pl.loop(0, members // 8)
    def _(index):
        group = pl.ds(pl.multiple_of(index * 8, 8), 8)
        coefs = coefficients(steps_ref, group)
        rows = spread_steps([field_ref[row, group, :] for row in range(lat)], coefs)
        square = jnp.zeros((8, lon), F32)
        cross = jnp.zeros((8, lon), F32)
        for row in range(lat):
            upper_ref[row, group, :] = rows[row]
            square = square + rows[row] * rows[row]
            if second:
                cross = cross + rows[row] * before_ref[row, group, :]
        dots_ref[0, group, :] = jnp.where(inside, square, 0.0)
        if second:
            dots_ref[1, group, :] = jnp.where(inside, cross, 0.0)
        rows = spread_steps(rows, coefs)
        for row in range(lat):
            lower_ref[row, group, :] = rows[row] * sigma_ref[pl.ds(row, 1), :]

    inside = inside[:1]
    for row in range(lat):
        high, low = split(jnp.where(inside, lower_ref[row], 0.0))
        halves[pl.ds(0, members), pl.ds(row * lon, lon)] = high
        halves[pl.ds(members, members), pl.ds(row * lon, lon)] = low
    width = own_ref.shape[0]
    for side, tile_ref in enumerate((own_ref, other_ref)):
        for start in range(0, width, 256):
            both = lax.dot_general(
                halves[...],
                tile_ref[pl.ds(start, 256), :],
                (((1,), (1,)), ((), ())),
                preferred_element_type=F32,
            )
            part_ref[:, pl.ds(side * width + start, 256)] = both[:members] + both[members:]


def interior(field, steps, sigma, own, other, before=None):
    lat, members, lon = field.shape
    more = () if before is None else (before,)
    shape = jax.ShapeDtypeStruct((lat, members, lon), F32)
    return pl.pallas_call(
        functools.partial(interior_kernel, before is not None),
        out_shape=(
            shape,
            shape,
            jax.ShapeDtypeStruct((1 + len(more), members, lon), F32),
            jax.ShapeDtypeStruct((members, 2 * own.shape[0]), F32),
        ),
        in_specs=[vmem()] * (5 + len(more)),
        out_specs=(vmem(),) * 4,
        scratch_shapes=[pltpu.VMEM((2 * members, lat * lon), BF16)],
        compiler_params=kernel_params(),
        cost_estimate=pl.CostEstimate(
            flops=8 * members * own.size, bytes_accessed=4 * own.size, transcendentals=0
        ),
        name="interior",
    )(field, steps, sigma, own, other, *more)


def interior_last_kernel(field_ref, steps_ref, upper_ref):
    lat, members, _ = field_ref.shape

    @pl.loop(0, members // 8)
    def _(index):
        group = pl.ds(pl.multiple_of(index * 8, 8), 8)
        rows = [field_ref[row, group, :] for row in range(lat)]
        rows = spread_steps(rows, coefficients(steps_ref, group))
        for row in range(lat):
            upper_ref[row, group, :] = rows[row]


def interior_last(field, steps):
    return pl.pallas_call(
        interior_last_kernel,
        out_shape=jax.ShapeDtypeStruct(field.shape, F32),
        in_specs=[vmem()] * 2,
        out_specs=vmem(),
        compiler_params=kernel_params(),
        cost_estimate=pl.CostEstimate(
            flops=1000 * field.size, bytes_accessed=8 * field.size, transcendentals=0
        ),
        name="interior_last",
    )(field, steps)


def strip_lanes(shape):
    lane = lax.broadcasted_iota(jnp.int32, shape, 1)
    second = ((lane >= 48) & (lane < 80)) | ((lane >= 80) & (lane < 112))
    first_a, last_a = (lane >= 32) & (lane < 40), lane >= 120
    first_b, last_b = (lane >= 96) & (lane < 104), (lane >= 56) & (lane < 64)
    return second, first_a | last_a, first_b | last_b


def strip_rows(field_ref, first_ref, last_ref, group_a, group_b):
    lat, _, lon = field_ref.shape
    gap = jnp.zeros((8, 16), F32)
    rows = []
    for row in range(lat):
        a, b = field_ref[row, group_a, :], field_ref[row, group_b, :]
        span = pl.ds(row * EDGE, EDGE)
        after_a, before_a = first_ref[group_a, span], last_ref[group_a, span]
        after_b, before_b = first_ref[group_b, span], last_ref[group_b, span]
        pieces = [after_a, gap, before_a, a[:, :16], b[:, lon - 16 :]]
        pieces = pieces + [after_b, gap, before_b, b[:, :16], a[:, lon - 16 :]]
        rows.append(jnp.concatenate(pieces, axis=1))
    return rows


def strip_coefficients(steps_ref, group_a, group_b, second):
    of_a, of_b = coefficients(steps_ref, group_a), coefficients(steps_ref, group_b)
    return [jnp.where(second, b, a) for a, b in zip(of_a, of_b)]


def strip_sigma(sigma):
    lane = lax.broadcasted_iota(jnp.int32, sigma.shape, 1)
    turned = [pltpu.roll(sigma, 32 * k, 1) if k else sigma for k in range(4)]
    return jnp.where(
        lane < 48, turned[1], jnp.where(lane < 80, turned[2], jnp.where(lane < 112, turned[3], turned[0]))
    )


def strips_kernel(second, target_ref, live_ref, *refs):
    field_ref, first_ref, last_ref, steps_ref, sigma_ref, own_ref, other_ref, part_ref, inner_ref = refs[:9]
    refs = refs[9:]
    if second:
        before_ref, refs = refs[0], refs[1:]
    upper_ref, lower_ref, dots_ref = refs[:3]
    pieces = refs[3 : 3 + OFFSETS]
    ends, sums = refs[3 + OFFSETS :]
    lat, members, lon = field_ref.shape
    obs = sums.shape[1]
    slots = own_ref.shape[0] // obs
    rows_each = sums.shape[0] // OFFSETS
    count = rows_each // members
    sigma = strip_sigma(sigma_ref[...])
    other_half, of_a, of_b = strip_lanes((8, lon))
    for pair in range(members // 16):
        group_a, group_b = pl.ds(pair * 16, 8), pl.ds(pair * 16 + 8, 8)
        here = pl.ds(pair * 8, 8)
        coefs = strip_coefficients(steps_ref, group_a, group_b, other_half)
        rows = spread_steps(strip_rows(field_ref, first_ref, last_ref, group_a, group_b), coefs)
        square = jnp.zeros((8, lon), F32)
        cross = jnp.zeros((8, lon), F32)
        for row in range(lat):
            upper_ref[row, here, :] = rows[row]
            square = square + rows[row] * rows[row]
            if second:
                cross = cross + rows[row] * before_ref[row, here, :]
        for k, value in enumerate((square, cross)[: 1 + second]):
            dots_ref[k, group_a, :] = inner_ref[k, group_a, :] + jnp.where(of_a, value, 0.0)
            dots_ref[k, group_b, :] = inner_ref[k, group_b, :] + jnp.where(of_b, value, 0.0)
        rows = spread_steps(rows, coefs)
        for row in range(lat):
            value = rows[row] * sigma[row : row + 1, :]
            lower_ref[row, here, :] = value
            begin = row * 2 * EDGE
            ends[group_a, pl.ds(begin, EDGE)] = value[:, 32:40]
            ends[group_a, pl.ds(begin + EDGE, EDGE)] = value[:, 120:]
            ends[group_b, pl.ds(begin, EDGE)] = value[:, 96:104]
            ends[group_b, pl.ds(begin + EDGE, EDGE)] = value[:, 56:64]
    high, low = split(ends[...])
    halves = jnp.concatenate([high, low], axis=0)
    sums[...] = jnp.zeros_like(sums)
    for side, tile_ref in enumerate((own_ref, other_ref)):
        both = lax.dot_general(
            halves, tile_ref[...], (((1,), (1,)), ((), ())), preferred_element_type=F32
        )
        total = both[:members] + both[members:]
        for slot in range(slots):
            target = target_ref[side, slot]
            place = (target // 2) * count + side * 2 + target % 2
            block = pl.ds(pl.multiple_of(place * members, members), members)
            inner = part_ref[:, pl.ds((side * slots + slot) * obs, obs)]
            value = total[:, slot * obs : (slot + 1) * obs] + inner
            sums[block, :] = sums[block, :] + value * live_ref[side, slot]
    for offset in range(OFFSETS):
        values = sums[pl.ds(offset * rows_each, rows_each), :]
        if offset == REACH:
            pieces[offset][...] = values
        else:
            encode_piece(pieces[offset], values)


def strips(targets, live, field, first, last, steps, sigma, own, other, part, inner, count, before=None):
    lat, members, lon = field.shape
    obs = own.shape[0] // targets.shape[1]
    more = () if before is None else (before,)
    shape = jax.ShapeDtypeStruct((lat, members // 2, lon), F32)
    pieces = [jax.ShapeDtypeStruct((count * members + EXTRA, obs), BF16) for _ in range(OFFSETS)]
    pieces[REACH] = jax.ShapeDtypeStruct((count * members, obs), F32)
    return pl.pallas_call(
        functools.partial(strips_kernel, before is not None),
        out_shape=(shape, shape, jax.ShapeDtypeStruct(inner.shape, F32), *pieces),
        in_specs=[smem(), smem()] + [vmem()] * (9 + len(more)),
        out_specs=(vmem(),) * (3 + OFFSETS),
        scratch_shapes=[
            pltpu.VMEM((members, lat * 2 * EDGE), F32),
            pltpu.VMEM((OFFSETS * count * members, obs), F32),
        ],
        compiler_params=kernel_params(),
        name="strips",
    )(targets, live, field, first, last, steps, sigma, own, other, part, inner, *more)


def weigh_kernel(*refs):
    pieces = refs[:OFFSETS]
    weight_ref, refs = refs[OFFSETS], refs[OFFSETS + 1 :]
    products = refs[:-3] if len(refs) > 3 else None
    coded_ref, plain_ref, row_ref = refs[-3:]
    count = weight_ref.shape[0]
    rows, obs = plain_ref.shape
    members = rows // count
    total = pieces[REACH][...]
    for offset in range(OFFSETS):
        if offset != REACH:
            total = total + decode_piece(pieces[offset], rows)
    weight = jnp.concatenate(
        [jnp.broadcast_to(weight_ref[pl.ds(block, 1), :], (members, obs)) for block in range(count)], axis=0
    )
    weighted = total * weight
    plain_ref[...] = weighted
    row_ref[...] = jnp.zeros_like(row_ref)
    row = None
    if products is not None:
        first_ref, second_ref = products
        curve = (total * weighted).reshape(count, members, obs)
        parts = jnp.concatenate(
            [first_ref[0], second_ref[1], second_ref[0], jnp.sum(curve, axis=0)], axis=0
        )
        row_ref[...] = lax.dot_general(
            jnp.ones((8, obs), F32),
            parts,
            (((1,), (1,)), ((), ())),
            precision=lax.Precision.HIGHEST,
            preferred_element_type=F32,
        )
        row = row_ref[pl.ds(0, 1), :]
    encode_piece(coded_ref, weighted, row)


def weigh(pieces, weight, *products):
    rows, obs = pieces[REACH].shape
    return pl.pallas_call(
        weigh_kernel,
        out_shape=(
            jax.ShapeDtypeStruct((rows + EXTRA, obs), BF16),
            jax.ShapeDtypeStruct((rows, obs), F32),
            jax.ShapeDtypeStruct((8, obs), F32),
        ),
        in_specs=[vmem()] * (OFFSETS + 1 + len(products)),
        out_specs=(vmem(),) * 3,
        compiler_params=kernel_params(),
        name="weigh",
    )(*pieces, weight, *products)


def finish_kernel(starts, field_ref, first_ref, last_ref, steps_ref, *refs):
    tails, refs = refs[: len(starts)], refs[len(starts) :]
    inner, ends, (increment_ref, residual_ref, dots) = refs[:5], refs[5:9], refs[9:]
    lat, members, lon = field_ref.shape
    row = jnp.zeros((8, dots.shape[0]), F32)
    for tail, (begin, parted) in zip(tails, starts):
        some = carried_row(tail, begin, 8) if parted else tail[pl.ds(begin, 8), pl.ds(0, lon)]
        row = row + some
    square = (dots.shape[0], dots.shape[0])
    diagonal = lax.broadcasted_iota(jnp.int32, square, 0) == lax.broadcasted_iota(jnp.int32, square, 1)
    dots[...] = jnp.sum(jnp.where(diagonal, row[0:1], 0.0), axis=1, keepdims=True)
    other_half, _, _ = strip_lanes((8, lon))
    lane = lax.broadcasted_iota(jnp.int32, (8, lon), 1)

    def factors(begin):
        pp, pg, gg, gh = [dots[pl.ds(begin + k * members, 8), :] for k in range(4)]
        step0 = pp / (pp + pg)
        u, w = 1.0 - step0, -step0
        norm1 = u * u * pp + 2.0 * u * w * pg + w * w * gg
        x = u + norm1 / pp
        curve = x * (x * pp + (x + w) * pg + w * gg) + w * (x * pg + (x + w) * gg + w * gh)
        step1 = norm1 / curve
        columns = (step0 + step1 * x, step1 * w, u - step1 * x, w - step1 * (x + w), -step1 * w)
        return [jnp.broadcast_to(column, (8, lon)) for column in columns]

    def joined(middle, end, turn_first, turn_last):
        first = pltpu.roll(end, turn_first, 1)
        last = pltpu.roll(end, turn_last, 1) if turn_last else end
        return jnp.where(lane < EDGE, first, jnp.where(lane >= lon - EDGE, last, middle))

    for pair in range(members // 16):
        group_a, group_b = pl.ds(pair * 16, 8), pl.ds(pair * 16 + 8, 8)
        here = pl.ds(pair * 8, 8)
        coefs = strip_coefficients(steps_ref, group_a, group_b, other_half)
        rows = spread_steps(strip_rows(field_ref, first_ref, last_ref, group_a, group_b), coefs)
        of_a, of_b = factors(pair * 16), factors(pair * 16 + 8)
        of_ends = [jnp.where(other_half, b, a) for a, b in zip(of_a, of_b)]

        def combine(parts, some):
            start, image, start_low, image_low, last = parts
            increment = some[0] * start_low + some[1] * image_low
            return increment, some[2] * start + some[3] * image + some[4] * last

        for row in range(lat):
            strip = combine([part[row, here, :] for part in ends] + [rows[row]], of_ends)
            for group, some, turns in ((group_a, of_a, (96, 0)), (group_b, of_b, (32, 64))):
                middle = combine([part[row, group, :] for part in inner], some)
                increment_ref[group, row, :] = joined(middle[0], strip[0], *turns)
                residual_ref[group, row, :] = joined(middle[1], strip[1], *turns)


def finish(field, first, last, steps, tails, inner, ends):
    lat, members, lon = field.shape
    out = jax.ShapeDtypeStruct((members, lat, lon), F32)
    starts = [place for _, *place in tails]
    return pl.pallas_call(
        functools.partial(finish_kernel, starts),
        out_shape=(out, out),
        in_specs=[vmem()] * (4 + len(tails) + len(inner) + len(ends)),
        out_specs=(vmem(), vmem()),
        scratch_shapes=[pltpu.VMEM((4 * members, 1), F32)],
        compiler_params=kernel_params(),
        name="finish",
    )(field, first, last, steps, *[part for part, *_ in tails], *inner, *ends)


def local(footprints, slot_target, slot_count, step_count, sigma, innovations, obs_weight):
    tiles = footprints[0, 0]
    slots, obs, lat, lon = tiles.shape
    blocks = innovations.shape[0]
    members = step_count.shape[0]
    count = 2 * blocks
    rows = count * members
    mine = lax.axis_index("obs").astype(jnp.int32).reshape(1)
    packet, kept, steps = prepare(mine, slot_target, slot_count, step_count, innovations, obs_weight)
    got = shifted(packet, "obs", 1)
    base = blocks * members
    weight = jnp.concatenate([packet[base : base + blocks], got[base : base + blocks]])
    facts = jnp.stack([packet[base + blocks], got[base + blocks]])
    targets = facts[:, :slots].astype(jnp.int32)
    live = facts[:, slots : 2 * slots]
    start_blocks = jnp.concatenate([kept, got[:base]]).astype(BF16)
    other, other_ends = flatten_tiles(shifted(tiles, "obs", 1))
    own, own_ends = flatten_tiles(in_hbm(tiles))

    def nearby(block, plain):
        return [plain if k == REACH else shifted(block, "flux", REACH - k) for k in range(OFFSETS)]

    def back(pieces, carry=False):
        field, first, last = adjoint(
            pieces, targets, live, own, other, sigma, count, members, carry
        )
        return field, shifted(first, "flux", -1), shifted(last, "flux", 1)

    def home(pieces):
        return [
            piece if k == REACH else shifted(piece, "flux", k - REACH) for k, piece in enumerate(pieces)
        ]

    def ahead(field, first, last, before=(None, None)):
        upper, lower, inner, part = interior(field, steps, sigma, own, other, before[0])
        upper_ends, lower_ends, dots, *pieces = strips(
            targets, live, field, first, last, steps, sigma, own_ends, other_ends, part, inner, count, before[1]
        )
        return (upper, upper_ends), (lower, lower_ends), dots, home(pieces)

    start, start_low, first_dots, pieces = ahead(*back(nearby(start_blocks, start_blocks)))
    coded, plain, _ = weigh(pieces, weight)
    image, image_low, dots, pieces = ahead(*back(nearby(coded, plain)), start)
    coded, plain, row = weigh(pieces, weight, first_dots, dots)
    pieces = nearby(coded, plain)
    if lax.axis_size("flux") == 8:
        tails = [(piece, rows, True) for k, piece in enumerate(pieces) if k != REACH]
        tails = tails + [(row, 0, False), (shifted(row, "flux", 4), 0, False)]
        field, first, last = back(pieces, True)
        tails = tails + [(first, members, False), (last, members, False)]
    else:
        tails = [(lax.psum(row, "flux"), 0, False)]
        field, first, last = back(pieces)
    upper = interior_last(field, steps)
    inner, ends = zip(start, image, start_low, image_low)
    return finish(field, first, last, steps, tails, inner + (upper,), ends)


def solution(mesh):
    return jax.shard_map(
        local,
        mesh=mesh,
        in_specs=(
            P(("group", "flux"), "obs", None, None, None, None),
            P(("group", "flux"), "obs", None),
            P(("group", "flux"), "obs"),
            P(("group", "obs")),
            P("group", "flux"),
            P(("group", "flux", "obs"), None, None),
            P(("group", "flux", "obs"), None),
        ),
        out_specs=(P(("group", "obs"), None, "flux"), P(("group", "obs"), None, "flux")),
        check_vma=False,
    )
```
